128 devices in a mesh: role: 2 (over x_lo), vocab: 64 (over x_hi, y, z, core).
Axes of the slice: x: 4 (x_hi: 2, x_lo: 2; x = x_hi * 2 + x_lo), y: 4, z: 4, core: 2. Of those that a mesh axis runs over, the one named last changes fastest.
Arguments:
- teacher_rows: bfloat16 [1024, 4096], P(None, 'role'), may hold values from -256 to 256
- teacher_head: bfloat16 [4096, 81920], P('role', 'vocab'), may hold values from -4 to 4
- student_rows: bfloat16 [1024, 5120], P(None, 'role'), may hold values from -256 to 256
- student_head: bfloat16 [5120, 81920], P('role', 'vocab'), may hold values from -2 to 2
- token_ids: int32 [1024], replicated, may hold values from 0 to 81919
- loss_mask: int32 [1024], replicated, may hold values 0 or 1
Outputs:
- total_loss: float32 [], replicated
- weight_grad: bfloat16 [5120, 81920], P('role', 'vocab')
- hidden_grad: bfloat16 [1024, 5120], P('vocab', 'role')
The draws below stay inside these ranges and needn't reach their ends.
All inputs are finite; a program needn't handle non-finite values.
Results may differ from the reference program's by a relative error of at most 0.0053.
Values may be sent and summed in bfloat16 or wider, within the bound.
A program may use at most 128 MiB of HBM per device.

```python
import math
import jax
import jax.numpy as jnp

D_T = 4096
D_S = 5120
TOKENS = 1024
VOCAB = 81920


TEACHER_SPAN = 0.72


STUDENT_SPAN = 0.36


ROW_BOUND = 256.0


TEACHER_BOUND = 4.0


STUDENT_BOUND = 2.0


def head_parts(key, salt, width, count, span):
    key = jax.random.fold_in(key, salt)
    k_base = jax.random.fold_in(key, 0)
    k_spread = jax.random.fold_in(key, 2)
    k_left = jax.random.fold_in(key, 3)
    k_right = jax.random.fold_in(key, 4)
    gauss = jnp.clip(jax.random.normal(k_base, (width, count), jnp.float32), -6.0, 6.0)
    base = gauss
    spread = jnp.exp(jax.random.uniform(k_spread, (count,), jnp.float32, 0.0, math.log(5.0)))
    left_cols = jax.random.randint(k_left, (8,), 0, count // 2)
    right_cols = jax.random.randint(k_right, (8,), count // 2, count)
    spread = spread.at[left_cols].set(5.0).at[right_cols].set(5.0)
    ramp = 0.6 + 0.8 * jnp.arange(count, dtype=jnp.float32) / count
    weight = base * (span / math.sqrt(width)) * (spread * ramp)[None, :]
    return weight


def rows_with_pairs(key, salt, width, tokens, low, high):
    key = jax.random.fold_in(key, salt + 1)
    k_rows = jax.random.fold_in(key, 0)
    k_scale = jax.random.fold_in(key, 2)
    gauss = jnp.clip(jax.random.normal(k_rows, (tokens, width), jnp.float32), -6.0, 6.0)
    base = gauss
    scale = jnp.exp(jax.random.uniform(k_scale, (tokens,), jnp.float32, math.log(low), math.log(high)))
    rows = base * scale[:, None]
    return rows


def draw_teacher_rows(key, part):
    rows = rows_with_pairs(key, 101, D_T, TOKENS, 0.1, 1.0)
    return jnp.clip(rows, -ROW_BOUND, ROW_BOUND).astype(jnp.bfloat16)


def draw_teacher_head(key, part):
    weight = head_parts(key, 101, D_T, VOCAB, TEACHER_SPAN)
    return jnp.clip(weight, -TEACHER_BOUND, TEACHER_BOUND).astype(jnp.bfloat16)


def draw_student_rows(key, part):
    rows = rows_with_pairs(key, 202, D_S, TOKENS, 0.1, 1.0)
    return jnp.clip(rows, -ROW_BOUND, ROW_BOUND).astype(jnp.bfloat16)


def draw_student_head(key, part):
    weight = head_parts(key, 202, D_S, VOCAB, STUDENT_SPAN)
    return jnp.clip(weight, -STUDENT_BOUND, STUDENT_BOUND).astype(jnp.bfloat16)


def touch_ends(drawn, own_key, least, largest):
    shape = drawn.shape
    spot = [jax.random.randint(jax.random.fold_in(own_key, axis), (), 0, shape[axis]) for axis in range(len(shape))]
    drawn = drawn.at[tuple(spot)].set(least)
    longest = shape.index(max(shape))
    spot[longest] = (spot[longest] + 1) % shape[longest]
    return drawn.at[tuple(spot)].set(largest)


def setup_inputs(seed: int = 0) -> dict:
    seeds = jax.random.split(jax.random.key(seed), 7)
    teacher_rows = draw_teacher_rows(jax.random.fold_in(seeds[6], 71), 0)
    teacher_head = draw_teacher_head(jax.random.fold_in(seeds[6], 71), 0)
    student_rows = draw_student_rows(jax.random.fold_in(seeds[6], 71), 0)
    student_head = draw_student_head(jax.random.fold_in(seeds[6], 71), 0)
    token_ids = touch_ends(jax.random.randint(seeds[4], (TOKENS,), 0, VOCAB), jax.random.fold_in(seeds[4], 1), 0, VOCAB - 1).astype(jnp.int32)
    loss_mask = touch_ends((jax.random.randint(seeds[5], (TOKENS,), 0, 4) < 3).astype(jnp.int32), jax.random.fold_in(seeds[5], 1), 0, 1)
    return {"teacher_rows": teacher_rows, "teacher_head": teacher_head, "student_rows": student_rows, "student_head": student_head, "token_ids": token_ids, "loss_mask": loss_mask}


TAU = 2.0
BETA = 0.5


def log_normalize(values):
    top = jnp.max(values, axis=1, keepdims=True)
    total = jnp.sum(jnp.exp(values - top), axis=1, keepdims=True)
    return values - top - jnp.log(total)


def reference(teacher_rows, teacher_head, student_rows, student_head, token_ids, loss_mask):
    teacher_logits = jnp.dot(teacher_rows, teacher_head, preferred_element_type=jnp.float32) / TAU
    student_logits = jnp.dot(student_rows, student_head, preferred_element_type=jnp.float32)
    teacher_log = log_normalize(teacher_logits)
    cooled_log = log_normalize(student_logits / TAU)
    student_log = log_normalize(student_logits)
    teacher_prob = jnp.exp(teacher_log)
    weight = loss_mask.astype(jnp.float32)[:, None]
    picked = (jnp.arange(VOCAB, dtype=jnp.int32)[None, :] == token_ids[:, None]).astype(jnp.float32)
    total_loss = jnp.sum(weight * (TAU * TAU * teacher_prob * (teacher_log - cooled_log) - BETA * picked * student_log))
    gradient = (weight * (TAU * (jnp.exp(cooled_log) - teacher_prob) + BETA * (jnp.exp(student_log) - picked))).astype(jnp.bfloat16)
    weight_grad = jnp.dot(student_rows.T, gradient, preferred_element_type=jnp.float32).astype(jnp.bfloat16)
    hidden_grad = jnp.dot(gradient, student_head.T, preferred_element_type=jnp.float32).astype(jnp.bfloat16)
    return total_loss, weight_grad, hidden_grad
```

```python
import functools

import jax
import jax.numpy as jnp
from jax import lax
from jax.experimental import pallas as pl
from jax.experimental.pallas import tpu as pltpu
from jax.sharding import PartitionSpec as P

TAU = 2.0
BETA = 0.5
MESH = pl.DeviceIdType.MESH
F32 = jnp.float32
BF16 = jnp.bfloat16

CHUNKS = 4
AHEAD = 2
TILE = 256
LEVELS = 32767.0
XH, Y, Z, CORES = 2, 4, 4, 2


def as_columns(rows_ref, columns_ref):
    columns_ref[...] = rows_ref[...].T


def stacked(rows):
    place = lax.broadcasted_iota(jnp.int32, (8, 128), 0)
    tile = jnp.zeros((8, 128), F32)
    for k, row in enumerate(rows):
        tile = jnp.where(place == k, row, tile)
    return tile


def merge(tiles):
    top_t = functools.reduce(jnp.maximum, [t[0:1] for t in tiles])
    top_s = functools.reduce(jnp.maximum, [t[1:2] for t in tiles])
    teacher = cooled = student = cross = picked = 0.0
    for t in tiles:
        down_t = t[0:1] - top_t
        down_s = (t[1:2] - top_s) * 0.5
        scale_t = jnp.exp(down_t)
        scale_s = jnp.exp(down_s)
        teacher = teacher + t[2:3] * scale_t
        cooled = cooled + t[3:4] * scale_s
        student = student + t[4:5] * (scale_s * scale_s)
        cross = cross + scale_t * (t[5:6] + (down_t - down_s) * t[2:3])
        picked = picked + t[6:7]
    return top_t, top_s, teacher, cooled, student, cross, picked


def kernel(
    ids_ref, mask_ref, trows_hbm, thead_hbm, srows_hbm, shead_hbm,
    loss_ref, wgrad_hbm, hgrad_ref,
    trows, thead, srows, shead, mine, theirs, qs, qr, scale_s, scale_r, scale_columns,
    pad, columns, stat_columns, st_z, st_y, st_c, st_x, grad, h32, h16, rc, z16, zr, yown, y16, yr, xown, x16, xr,
    wtile, loss_row, loss_all,
    load_sem, q_sem, scale_sem, stz_sem, sty_sem, stc_sem, stx_sem, grad_sem, core_sem, z_sem, y_send, y_recv, x_sem,
    loss_sem, out_sem,
):
    r = lax.axis_index("role")
    v = lax.axis_index("vocab")
    core, z, y, xh = v % CORES, (v // 2) % Z, (v // 8) % Y, v // 32
    half = mine.shape[2]
    width = mine.shape[3]
    chunk = 2 * half
    model = shead.shape[0]
    tiles = width // TILE
    slab_start = v * width

    def at(role=r, x_hi=xh, yy=y, zz=z, cc=core):
        return (role, ((x_hi * Y + yy) * Z + zz) * CORES + cc)

    partner = at(role=1 - r)
    other_core = at(cc=1 - core)
    other_x = at(x_hi=1 - xh)

    def z_peer(k):
        return at(zz=(z + k) % Z)

    def y_peer(k):
        return at(yy=(y + k) % Y)

    def remote(src, dst, send, recv, device):
        return pltpu.make_async_remote_copy(
            src_ref=src, dst_ref=dst, send_sem=send, recv_sem=recv, device_id=device, device_id_type=MESH
        )

    sent = []

    def load_rows(m, first):
        hbm, ref = ((trows_hbm, trows), (srows_hbm, srows))[m]
        part = pl.ds(0, chunk) if first else pl.ds(chunk, ref.shape[0] - chunk)
        return pltpu.make_async_copy(hbm.at[part], ref.at[part], load_sem.at[m, tiles + (0 if first else 1)])

    def load_head(m, n):
        hbm, ref = ((thead_hbm, thead), (shead_hbm, shead))[m]
        part = pl.ds(pl.multiple_of(n * TILE, TILE), TILE)
        return pltpu.make_async_copy(hbm.at[:, part], ref.at[:, part], load_sem.at[m, n])

    for m in range(2):
        load_rows(m, True).start()
        for n in range(tiles):
            load_head(m, n).start()
    for m in range(2):
        load_rows(m, False).start()

    barrier = pltpu.get_barrier_semaphore()
    peers = [partner, other_core, other_x] + [z_peer(k) for k in (1, 2, 3)] + [y_peer(k) for k in (1, 2, 3)]
    for peer in peers:
        pl.semaphore_signal(barrier, inc=1, device_id=peer, device_id_type=MESH)

    pad[...] = jnp.zeros_like(pad)
    scale_columns[...] = jnp.zeros_like(scale_columns)
    stat_columns[...] = jnp.zeros_like(stat_columns)
    loss_row[...] = jnp.zeros_like(loss_row)

    def q_copy(c, m):
        return remote(qs.at[c, m], qr.at[c, m], q_sem.at[0, c, m], q_sem.at[1, c, m], partner)

    def scale_copy(c):
        return remote(scale_s.at[c], scale_r.at[c], scale_sem.at[0, c], scale_sem.at[1, c], partner)

    def logits(c):
        for m, (rows, head) in enumerate(((trows, thead), (srows, shead))):
            if c < 2:
                load_rows(m, c == 0).wait()

            @pl.loop(0, tiles)
            def _(n):
                if c == 0:
                    load_head(m, n).wait()
                part = pl.ds(pl.multiple_of(n * TILE, TILE), TILE)
                product = jnp.dot(rows[pl.ds(c * chunk, chunk), :], head[:, part], preferred_element_type=F32)
                low, high = product[:half], product[half:]
                mine[c, m, :, part] = jnp.where(r == 0, low, high)
                theirs[m, :, part] = jnp.where(r == 0, high, low)

            @pl.loop(0, half // 16)
            def _(b):
                part = pl.ds(pl.multiple_of(b * 16, 16), 16)
                x = theirs[m, part, :]
                top = jnp.maximum(jnp.max(jnp.abs(x), axis=1, keepdims=True), 1e-30)
                qs[c, m, part, :] = jnp.round(x * (LEVELS / top)).astype(jnp.int32).astype(jnp.int16)
                scale_columns[part, m : m + 1] = top * (1.0 / LEVELS)

            if c == 0 and m == 0:
                pl.semaphore_wait(barrier, len(peers))
            q_copy(c, m).start()
            sent.append(q_copy(c, m))
        scale_s[c] = scale_columns[...].T[0:8]
        scale_copy(c).start()
        sent.append(scale_copy(c))

    def spread(ref, sems, c, me, peer):
        copies = [
            remote(ref.at[c, me], ref.at[c, me], sems.at[0, c, k], sems.at[1, c, k], d) for k, d in enumerate(peer)
        ]
        for copy in copies:
            copy.start()
        sent.extend(copies)
        return copies

    def joined(ref, c, copies):
        for copy in copies:
            copy.wait_recv()
        return merge([ref[c, i] for i in range(ref.shape[1])])

    def local_stats(c):
        scale_copy(c).wait_recv()
        for m in range(2):
            q_copy(c, m).wait_recv()
        pad[0:8, :] = scale_r[c]
        pad[8:9, :] = ids_ref[pl.ds(2 * c + r, 1), :].astype(F32)
        as_columns(pad, columns)

        @pl.loop(0, half // 16)
        def _(b):
            part = pl.ds(pl.multiple_of(b * 16, 16), 16)
            got_t = qr[c, 0, part, :].astype(jnp.int32).astype(F32) * columns[part, 0:1]
            got_s = qr[c, 1, part, :].astype(jnp.int32).astype(F32) * columns[part, 1:2]
            t = (mine[c, 0, part, :] + got_t) * (1.0 / TAU)
            s = mine[c, 1, part, :] + got_s
            label = columns[part, 8:9].astype(jnp.int32)
            place = lax.broadcasted_iota(jnp.int32, s.shape, 1) + slab_start
            top_t = jnp.max(t, axis=1, keepdims=True)
            top_s = jnp.max(s, axis=1, keepdims=True)
            down_t = t - top_t
            down_s = (s - top_s) * (1.0 / TAU)
            exp_t = jnp.exp(down_t)
            exp_s = jnp.exp(down_s)
            mine[c, 0, part, :] = exp_t
            mine[c, 1, part, :] = exp_s
            sums = (
                top_t,
                top_s,
                jnp.sum(exp_t, axis=1, keepdims=True),
                jnp.sum(exp_s, axis=1, keepdims=True),
                jnp.sum(exp_s * exp_s, axis=1, keepdims=True),
                jnp.sum(exp_t * (down_t - down_s), axis=1, keepdims=True),
                jnp.sum(jnp.where(place == label, s, 0.0), axis=1, keepdims=True),
            )
            for k, value in enumerate(sums):
                stat_columns[part, k : k + 1] = value

        tile = stat_columns[...].T[0:8]
        st_z[c, z] = tile
        return tile[0:1], tile[1:2], spread(st_z, stz_sem, c, z, [z_peer(k) for k in (1, 2, 3)])

    def grad_copy(c, h):
        block = grad.at[2 * c + h]
        return remote(block, block, grad_sem.at[0, c], grad_sem.at[1, c], partner)

    def gradient(c, own_t, own_s, stats):
        top_t, top_s, teacher, cooled, student, cross, picked = stats
        mask = mask_ref[pl.ds(2 * c + r, 1), :].astype(F32)
        down_s = jnp.exp((own_s - top_s) * 0.5)
        pad[0:8, :] = stacked([
            TAU * mask * (down_s / cooled),
            TAU * mask * (jnp.exp(own_t - top_t) / teacher),
            BETA * mask * (down_s * down_s / student),
            BETA * mask,
        ])
        as_columns(pad, columns)
        loss_row[...] += mask * (
            TAU * TAU * (cross / teacher - jnp.log(teacher) + jnp.log(cooled))
            - BETA * (picked - top_s - jnp.log(student))
        )

        @pl.loop(0, half // 16)
        def _(b):
            part = pl.ds(pl.multiple_of(b * 16, 16), 16)
            exp_t = mine[c, 0, part, :]
            exp_s = mine[c, 1, part, :]
            label = columns[part, 8:9].astype(jnp.int32)
            place = lax.broadcasted_iota(jnp.int32, exp_s.shape, 1) + slab_start
            g = exp_s * (columns[part, 0:1] + columns[part, 2:3] * exp_s) - exp_t * columns[part, 1:2]
            g = g - jnp.where(place == label, columns[part, 3:4], 0.0)
            grad[2 * c + r, part, :] = g.astype(BF16)

        grad_copy(c, r).start()
        sent.append(grad_copy(c, r))

    def core_copy(g, slot):
        return remote(h16.at[slot, :, 1 - core], rc.at[g], core_sem.at[0, g], core_sem.at[1, g], other_core)

    def z_copies(g, slot):
        return [
            remote(z16.at[slot, (z + k) % Z], zr.at[g, k - 1], z_sem.at[0, g, k - 1], z_sem.at[1, g, k - 1], z_peer(k))
            for k in (1, 2, 3)
        ]

    def y_copy(g):
        hop = (g % Y - y + Y) % Y
        return remote(y16.at[g], yr.at[g // Y, hop - 1], y_send.at[g], y_recv.at[g // Y, hop - 1], at(yy=g % Y))

    x_copy = remote(x16, xr, x_sem.at[0], x_sem.at[1], other_x)
    busy = {}

    def hidden(c, h, slot):
        g = 2 * c + h
        for copy in busy.pop(("core", slot), []):
            copy.wait_send()

        @pl.loop(0, model // 512)
        def _(n):
            part = pl.ds(pl.multiple_of(n * 512, 512), 512)
            product = lax.dot_general(
                grad[g], shead[part, :], (((1,), (1,)), ((), ())), preferred_element_type=F32
            ).reshape(Z, CORES, 16, 512)
            h32[slot, :, :, :, part] = product
            h16[slot, :, :, :, part] = product.astype(BF16)

        core_copy(g, slot).start()
        busy["core", slot] = [core_copy(g, slot)]

    def over_z(c, h, slot):
        g = 2 * c + h
        core_copy(g, slot).wait_recv()
        for copy in busy.pop(("z", slot), []):
            copy.wait_send()

        @pl.loop(0, Z)
        def _(i):
            total = h32[slot, i, core] + rc[g, i].astype(F32)
            h32[slot, i, core] = total
            z16[slot, i] = total.astype(BF16)

        for copy in z_copies(g, slot):
            copy.start()
        busy["z", slot] = z_copies(g, slot)

    def over_y(c, h, slot):
        g = 2 * c + h
        for copy in z_copies(g, slot):
            copy.wait_recv()
        total = h32[slot, z, core]
        for k in range(Z - 1):
            total = total + zr[g, k].astype(F32)
        y16[g] = total.astype(BF16)

        @pl.when(y == g % Y)
        def _():
            yown[g // Y] = total

        @pl.when(y != g % Y)
        def _():
            y_copy(g).start()

    def over_x(c, h):
        g = 2 * c + h

        @pl.when(y == g % Y)
        def _():
            total = yown[g // Y]
            for k in range(Y - 1):
                remote(
                    y16.at[g], yr.at[g // Y, k], y_send.at[g], y_recv.at[g // Y, k], partner
                ).wait_recv()
            for k in range(Y - 1):
                total = total + yr[g // Y, k].astype(F32)

            @pl.when(xh == g // Y)
            def _():
                xown[...] = total

            @pl.when(xh != g // Y)
            def _():
                x16[...] = total.astype(BF16)
                x_copy.start()

    def weight_tiles(first, last):
        @pl.loop(first, last)
        def _(f):
            part = pl.ds(pl.multiple_of(f * TILE, TILE), TILE)
            product = lax.dot_general(
                srows[:, part], grad[...].reshape(2 * CHUNKS * half, width),
                (((0,), (0,)), ((), ())), preferred_element_type=F32,
            )
            wtile[f] = product.astype(BF16)
            pltpu.make_async_copy(wtile.at[f], wgrad_hbm.at[part], out_sem.at[f]).start()

    own, other = r, 1 - r
    for c in range(AHEAD):
        logits(c)
    for c in range(CHUNKS):
        own_t, own_s, copies = local_stats(c)
        if c + AHEAD < CHUNKS:
            logits(c + AHEAD)
        st_y[c, y] = stacked(joined(st_z, c, copies))
        copies = spread(st_y, sty_sem, c, y, [y_peer(k) for k in (1, 2, 3)])
        if c > 0:
            hidden(c - 1, own, 0)
        st_c[c, core] = stacked(joined(st_y, c, copies))
        copies = spread(st_c, stc_sem, c, core, [other_core])
        if c > 0:
            grad_copy(c - 1, other).wait_recv()
            hidden(c - 1, other, 1)
        st_x[c, xh] = stacked(joined(st_c, c, copies))
        copies = spread(st_x, stx_sem, c, xh, [other_x])
        if c > 0:
            over_z(c - 1, own, 0)
            over_z(c - 1, other, 1)
        gradient(c, own_t, own_s, joined(st_x, c, copies))
        if c > 0:
            over_y(c - 1, own, 0)
            over_y(c - 1, other, 1)
            over_x(c - 1, own)
            over_x(c - 1, other)

    last = CHUNKS - 1
    loss_all[r] = jnp.broadcast_to(loss_row[...], (8, 128))
    loss_copy = remote(loss_all.at[r], loss_all.at[r], loss_sem.at[0], loss_sem.at[1], partner)
    loss_copy.start()
    hidden(last, own, 0)
    over_z(last, own, 0)
    over_y(last, own, 0)
    grad_copy(last, other).wait_recv()
    hidden(last, other, 1)
    n_f = model // TILE
    weight_tiles(0, 3)
    over_z(last, other, 1)
    over_x(last, own)
    weight_tiles(3, 6)
    over_y(last, other, 1)
    weight_tiles(6, 8)
    over_x(last, other)
    weight_tiles(8, n_f)
    x_copy.wait_recv()
    hgrad_ref[...] = (xown[...] + xr[...].astype(F32)).astype(BF16)
    loss_copy.wait_recv()
    loss_ref[...] = jnp.sum(loss_all[0, 0:1, :] + loss_all[1, 0:1, :], axis=1, keepdims=True)

    loss_copy.wait_send()
    x_copy.wait_send()
    for copies in busy.values():
        for copy in copies:
            copy.wait_send()
    for copy in sent:
        copy.wait_send()
    for g in range(2 * CHUNKS):
        @pl.when(y != g % Y)
        def _():
            y_copy(g).wait_send()

    @pl.loop(0, n_f)
    def _(f):
        part = pl.ds(pl.multiple_of(f * TILE, TILE), TILE)
        pltpu.make_async_copy(wtile.at[f], wgrad_hbm.at[part], out_sem.at[f]).wait()


def shards(teacher_rows, teacher_head, student_rows, student_head, token_ids, loss_mask):
    tokens, d_t = teacher_rows.shape
    d_s, width = student_head.shape
    half = tokens // (2 * CHUNKS)
    blocks = 2 * CHUNKS
    vmem = pl.BlockSpec(memory_space=pltpu.VMEM)
    anywhere = pl.BlockSpec(memory_space=pl.ANY)
    dma = pltpu.SemaphoreType.DMA
    tiles = width // TILE
    loss, wgrad, hgrad = pl.pallas_call(
        kernel,
        out_shape=(
            jax.ShapeDtypeStruct((1, 1), F32),
            jax.ShapeDtypeStruct((d_s, width), BF16),
            jax.ShapeDtypeStruct((16, d_s), BF16),
        ),
        in_specs=[vmem, vmem, anywhere, anywhere, anywhere, anywhere],
        out_specs=(vmem, anywhere, vmem),
        scratch_shapes=[
            pltpu.VMEM((tokens, d_t), BF16),
            pltpu.VMEM((d_t, width), BF16),
            pltpu.VMEM((tokens, d_s), BF16),
            pltpu.VMEM((d_s, width), BF16),
            pltpu.VMEM((CHUNKS, 2, half, width), F32),
            pltpu.VMEM((2, half, width), F32),
            pltpu.VMEM((CHUNKS, 2, half, width), jnp.int16),
            pltpu.VMEM((CHUNKS, 2, half, width), jnp.int16),
            pltpu.VMEM((CHUNKS, 8, 128), F32),
            pltpu.VMEM((CHUNKS, 8, 128), F32),
            pltpu.VMEM((128, 128), F32),
            pltpu.VMEM((128, 128), F32),
            pltpu.VMEM((128, 128), F32),
            pltpu.VMEM((128, 128), F32),
            pltpu.VMEM((CHUNKS, Z, 8, 128), F32),
            pltpu.VMEM((CHUNKS, Y, 8, 128), F32),
            pltpu.VMEM((CHUNKS, CORES, 8, 128), F32),
            pltpu.VMEM((CHUNKS, XH, 8, 128), F32),
            pltpu.VMEM((blocks, half, width), BF16),
            pltpu.VMEM((2, Z, CORES, 16, d_s), F32),
            pltpu.VMEM((2, Z, CORES, 16, d_s), BF16),
            pltpu.VMEM((blocks, Z, 16, d_s), BF16),
            pltpu.VMEM((2, Z, 16, d_s), BF16),
            pltpu.VMEM((blocks, Z - 1, 16, d_s), BF16),
            pltpu.VMEM((XH, 16, d_s), F32),
            pltpu.VMEM((blocks, 16, d_s), BF16),
            pltpu.VMEM((XH, Y - 1, 16, d_s), BF16),
            pltpu.VMEM((16, d_s), F32),
            pltpu.VMEM((16, d_s), BF16),
            pltpu.VMEM((16, d_s), BF16),
            pltpu.VMEM((d_s // TILE, TILE, width), BF16),
            pltpu.VMEM((1, 128), F32),
            pltpu.VMEM((2, 8, 128), F32),
            dma((2, tiles + 2)),
            dma((2, CHUNKS, 2)),
            dma((2, CHUNKS)),
            dma((2, CHUNKS, Z - 1)),
            dma((2, CHUNKS, Y - 1)),
            dma((2, CHUNKS, CORES - 1)),
            dma((2, CHUNKS, XH - 1)),
            dma((2, CHUNKS)),
            dma((2, blocks)),
            dma((2, blocks, Z - 1)),
            dma((blocks,)),
            dma((XH, Y - 1)),
            dma((2,)),
            dma((2,)),
            dma((d_s // TILE,)),
        ],
        compiler_params=pltpu.CompilerParams(
            collective_id=0, has_side_effects=True, vmem_limit_bytes=60 << 20
        ),
        cost_estimate=pl.CostEstimate(flops=26_000_000_000, bytes_accessed=28_000_000, transcendentals=2_000_000),
        name="distill",
    )(
        token_ids.reshape(tokens // 128, 128),
        loss_mask.reshape(tokens // 128, 128),
        teacher_rows,
        teacher_head,
        student_rows,
        student_head,
    )
    return loss.reshape(()), wgrad, hgrad


def solution(mesh):
    placed = (P(None, "role"), P("role", "vocab"), P(None, "role"), P("role", "vocab"), P(), P())
    return jax.shard_map(
        shards,
        mesh=mesh,
        in_specs=placed,
        out_specs=(P(), P("role", "vocab"), P("vocab", "role")),
        check_vma=False,
    )
```

```python
import functools

import jax
import jax.numpy as jnp
from jax import lax
from jax.experimental import pallas as pl
from jax.experimental.pallas import tpu as pltpu
from jax.sharding import PartitionSpec as P

TAU = 2.0
BETA = 0.5
MESH = pl.DeviceIdType.MESH
F32 = jnp.float32
BF16 = jnp.bfloat16

CHUNKS = 4
AHEAD = 2
TILE = 256
LEVELS = 32767.0
XH, Y, Z, CORES = 2, 4, 4, 2
SLOTS = 3
PARTS = 2
HIDDEN_TILE = 640
W_SLOTS = 5


def as_columns(rows_ref, columns_ref):
    columns_ref[...] = rows_ref[...].T


def stacked(rows):
    place = lax.broadcasted_iota(jnp.int32, (8, 128), 0)
    tile = jnp.zeros((8, 128), F32)
    for k, row in enumerate(rows):
        tile = jnp.where(place == k, row, tile)
    return tile


def merge(tiles):
    top_t = functools.reduce(jnp.maximum, [t[0:1] for t in tiles])
    top_s = functools.reduce(jnp.maximum, [t[1:2] for t in tiles])
    teacher = cooled = student = cross = picked = 0.0
    for t in tiles:
        down_t = t[0:1] - top_t
        down_s = (t[1:2] - top_s) * 0.5
        scale_t = jnp.exp(down_t)
        scale_s = jnp.exp(down_s)
        teacher = teacher + t[2:3] * scale_t
        cooled = cooled + t[3:4] * scale_s
        student = student + t[4:5] * (scale_s * scale_s)
        cross = cross + scale_t * (t[5:6] + (down_t - down_s) * t[2:3])
        picked = picked + t[6:7]
    return top_t, top_s, teacher, cooled, student, cross, picked


def kernel(
    ids_ref, mask_ref, trows_hbm, thead_hbm, srows_hbm, shead_hbm,
    loss_ref, wgrad_hbm, hgrad_ref,
    trows, thead, srows, shead, mine, theirs, qs, qr, scale_s, scale_r, scale_columns,
    pad, columns, stat_columns, st_z, st_y, st_c, st_x, grad, h32, h16, rc, z16, zr, yown, y16, yr, xown, x16, xr,
    wtile, loss_row, loss_all,
    load_sem, q_sem, scale_sem, stz_sem, sty_sem, stc_sem, stx_sem, grad_sem, core_sem, z_sem, y_send, y_recv, x_sem,
    loss_sem, out_sem,
):
    r = lax.axis_index("role")
    v = lax.axis_index("vocab")
    core, z, y, xh = v % CORES, (v // 2) % Z, (v // 8) % Y, v // 32
    half = mine.shape[2]
    width = mine.shape[3]
    chunk = 2 * half
    model = shead.shape[0]
    tiles = width // TILE
    slab_start = v * width

    def at(role=r, x_hi=xh, yy=y, zz=z, cc=core):
        return (role, ((x_hi * Y + yy) * Z + zz) * CORES + cc)

    partner = at(role=1 - r)
    other_core = at(cc=1 - core)
    other_x = at(x_hi=1 - xh)
    side = (r + xh) % 2
    facing = at(role=1 - r, x_hi=1 - xh)

    def z_peer(k):
        return at(zz=(z + k) % Z)

    def y_peer(k):
        return at(yy=(y + k) % Y)

    def remote(src, dst, send, recv, device):
        return pltpu.make_async_remote_copy(
            src_ref=src, dst_ref=dst, send_sem=send, recv_sem=recv, device_id=device, device_id_type=MESH
        )

    sent = []

    def load_rows(m, first):
        hbm, ref = ((trows_hbm, trows), (srows_hbm, srows))[m]
        part = pl.ds(0, chunk) if first else pl.ds(chunk, ref.shape[0] - chunk)
        return pltpu.make_async_copy(hbm.at[part], ref.at[part], load_sem.at[m, tiles + (0 if first else 1)])

    def load_head(m, n):
        hbm, ref = ((thead_hbm, thead), (shead_hbm, shead))[m]
        part = pl.ds(pl.multiple_of(n * TILE, TILE), TILE)
        return pltpu.make_async_copy(hbm.at[:, part], ref.at[:, part], load_sem.at[m, n])

    for m in range(2):
        load_rows(m, True).start()
        for n in range(tiles):
            load_head(m, n).start()
    for m in range(2):
        load_rows(m, False).start()

    barrier = pltpu.get_barrier_semaphore()
    peers = [partner, other_core, other_x, facing] + [z_peer(k) for k in (1, 2, 3)] + [y_peer(k) for k in (1, 2, 3)]
    for peer in peers:
        pl.semaphore_signal(barrier, inc=1, device_id=peer, device_id_type=MESH)

    pad[...] = jnp.zeros_like(pad)
    scale_columns[...] = jnp.zeros_like(scale_columns)
    stat_columns[...] = jnp.zeros_like(stat_columns)
    loss_row[...] = jnp.zeros_like(loss_row)

    def q_copy(c, m):
        return remote(qs.at[c, m], qr.at[c, m], q_sem.at[0, c, m], q_sem.at[1, c, m], partner)

    def scale_copy(c):
        return remote(scale_s.at[c], scale_r.at[c], scale_sem.at[0, c], scale_sem.at[1, c], partner)

    def logits(c):
        for m, (rows, head) in enumerate(((trows, thead), (srows, shead))):
            if c < 2:
                load_rows(m, c == 0).wait()

            @pl.loop(0, tiles)
            def _(n):
                if c == 0:
                    load_head(m, n).wait()
                part = pl.ds(pl.multiple_of(n * TILE, TILE), TILE)
                product = jnp.dot(rows[pl.ds(c * chunk, chunk), :], head[:, part], preferred_element_type=F32)
                low, high = product[:half], product[half:]
                mine[c, m, :, part] = jnp.where(side == 0, low, high)
                theirs[m, :, part] = jnp.where(side == 0, high, low)

            @pl.loop(0, half // 16)
            def _(b):
                part = pl.ds(pl.multiple_of(b * 16, 16), 16)
                x = theirs[m, part, :]
                top = jnp.maximum(jnp.max(jnp.abs(x), axis=1, keepdims=True), 1e-30)
                qs[c, m, part, :] = jnp.round(x * (LEVELS / top)).astype(jnp.int32).astype(jnp.int16)
                scale_columns[part, m : m + 1] = top * (1.0 / LEVELS)

            if c == 0 and m == 0:
                pl.semaphore_wait(barrier, len(peers))
            q_copy(c, m).start()
            sent.append(q_copy(c, m))
        scale_s[c] = scale_columns[...].T[0:8]
        scale_copy(c).start()
        sent.append(scale_copy(c))

    def spread(ref, sems, c, me, peer):
        copies = [
            remote(ref.at[c, me], ref.at[c, me], sems.at[0, c, k], sems.at[1, c, k], d) for k, d in enumerate(peer)
        ]
        for copy in copies:
            copy.start()
        sent.extend(copies)
        return copies

    def joined(ref, c, copies):
        for copy in copies:
            copy.wait_recv()
        return merge([ref[c, i] for i in range(ref.shape[1])])

    def local_stats(c):
        scale_copy(c).wait_recv()
        for m in range(2):
            q_copy(c, m).wait_recv()
        pad[0:8, :] = scale_r[c]
        pad[8:9, :] = ids_ref[pl.ds(2 * c + side, 1), :].astype(F32)
        as_columns(pad, columns)

        @pl.loop(0, half // 16)
        def _(b):
            part = pl.ds(pl.multiple_of(b * 16, 16), 16)
            got_t = qr[c, 0, part, :].astype(jnp.int32).astype(F32) * columns[part, 0:1]
            got_s = qr[c, 1, part, :].astype(jnp.int32).astype(F32) * columns[part, 1:2]
            t = (mine[c, 0, part, :] + got_t) * (1.0 / TAU)
            s = mine[c, 1, part, :] + got_s
            label = columns[part, 8:9].astype(jnp.int32)
            place = lax.broadcasted_iota(jnp.int32, s.shape, 1) + slab_start
            top_t = jnp.max(t, axis=1, keepdims=True)
            top_s = jnp.max(s, axis=1, keepdims=True)
            down_t = t - top_t
            down_s = (s - top_s) * (1.0 / TAU)
            exp_t = jnp.exp(down_t)
            exp_s = jnp.exp(down_s)
            mine[c, 0, part, :] = exp_t
            mine[c, 1, part, :] = exp_s
            sums = (
                top_t,
                top_s,
                jnp.sum(exp_t, axis=1, keepdims=True),
                jnp.sum(exp_s, axis=1, keepdims=True),
                jnp.sum(exp_s * exp_s, axis=1, keepdims=True),
                jnp.sum(exp_t * (down_t - down_s), axis=1, keepdims=True),
                jnp.sum(jnp.where(place == label, s, 0.0), axis=1, keepdims=True),
            )
            for k, value in enumerate(sums):
                stat_columns[part, k : k + 1] = value

        tile = stat_columns[...].T[0:8]
        st_z[c, z] = tile
        return tile[0:1], tile[1:2], spread(st_z, stz_sem, c, z, [z_peer(k) for k in (1, 2, 3)])

    def grad_copy(c, h):
        block = grad.at[2 * c + h]
        return remote(block, block, grad_sem.at[0, c], grad_sem.at[1, c], partner)

    def gradient(c, own_t, own_s, stats):
        top_t, top_s, teacher, cooled, student, cross, picked = stats
        mask = mask_ref[pl.ds(2 * c + side, 1), :].astype(F32)
        down_s = jnp.exp((own_s - top_s) * 0.5)
        pad[0:8, :] = stacked([
            TAU * mask * (down_s / cooled),
            TAU * mask * (jnp.exp(own_t - top_t) / teacher),
            BETA * mask * (down_s * down_s / student),
            BETA * mask,
        ])
        as_columns(pad, columns)
        loss_row[...] += mask * (
            TAU * TAU * (cross / teacher - jnp.log(teacher) + jnp.log(cooled))
            - BETA * (picked - top_s - jnp.log(student))
        )

        @pl.loop(0, half // 16)
        def _(b):
            part = pl.ds(pl.multiple_of(b * 16, 16), 16)
            exp_t = mine[c, 0, part, :]
            exp_s = mine[c, 1, part, :]
            label = columns[part, 8:9].astype(jnp.int32)
            place = lax.broadcasted_iota(jnp.int32, exp_s.shape, 1) + slab_start
            g = exp_s * (columns[part, 0:1] + columns[part, 2:3] * exp_s) - exp_t * columns[part, 1:2]
            g = g - jnp.where(place == label, columns[part, 3:4], 0.0)
            grad[2 * c + side, part, :] = g.astype(BF16)

        grad_copy(c, side).start()
        sent.append(grad_copy(c, side))

    def span(p):
        return pl.ds(p * (model // PARTS), model // PARTS)

    def slot_of(c, h):
        return 2 * (c % SLOTS) + h

    def core_copy(c, h, p):
        g = 2 * c + h
        return remote(
            h16.at[slot_of(c, h), :, :, span(p)], rc.at[g, :, :, span(p)],
            core_sem.at[0, g, p], core_sem.at[1, g, p], other_core,
        )

    def z_copies(c, h, p):
        g = 2 * c + h
        return [
            remote(
                z16.at[slot_of(c, h), (z + k) % Z, :, span(p)], zr.at[g, k - 1, :, span(p)],
                z_sem.at[0, g, p, k - 1], z_sem.at[1, g, p, k - 1], z_peer(k),
            )
            for k in (1, 2, 3)
        ]

    def y_copy(g, p):
        hop = (g % Y - y + Y) % Y
        return remote(
            y16.at[g, :, span(p)], yr.at[g // Y, hop - 1, :, span(p)],
            y_send.at[g, p], y_recv.at[g // Y, hop - 1, p], at(yy=g % Y),
        )

    def x_copy(p):
        return remote(x16.at[:, span(p)], xr.at[:, span(p)], x_sem.at[0, p], x_sem.at[1, p], other_x)

    def hidden(c, h, count):
        g = 2 * c + h
        if c >= SLOTS:
            for i in range(count):
                for p in range(PARTS):
                    core_copy(c - SLOTS, h + i, p).wait_send()
        wide = HIDDEN_TILE
        for p in range(PARTS):
            @pl.loop(0, model // PARTS // wide)
            def _(n):
                part = pl.ds(pl.multiple_of(p * (model // PARTS) + n * wide, 128), wide)
                product = lax.dot_general(
                    grad[pl.ds(g, count)].reshape(count * half, width), shead[part, :],
                    (((1,), (1,)), ((), ())), preferred_element_type=F32,
                ).reshape(count, Z, CORES, 16, wide)
                for i in range(count):
                    first, second = product[i, :, 0], product[i, :, 1]
                    slot = slot_of(c, h) + i
                    h32[slot, :, :, part] = jnp.where(core == 0, first, second)
                    h16[slot, :, :, part] = jnp.where(core == 0, second, first).astype(BF16)

            for i in range(count):
                core_copy(c, h + i, p).start()

    def over_z(c, h):
        g = 2 * c + h
        slot = slot_of(c, h)
        for p in range(PARTS):
            core_copy(c, h, p).wait_recv()
            if c >= SLOTS:
                for copy in z_copies(c - SLOTS, h, p):
                    copy.wait_send()

            @pl.loop(0, Z)
            def _(i):
                total = h32[slot, i, :, span(p)] + rc[g, i, :, span(p)].astype(F32)
                h32[slot, i, :, span(p)] = total
                z16[slot, i, :, span(p)] = total.astype(BF16)

            for copy in z_copies(c, h, p):
                copy.start()

    def over_y(c, h):
        g = 2 * c + h
        for p in range(PARTS):
            for copy in z_copies(c, h, p):
                copy.wait_recv()
            total = h32[slot_of(c, h), z, :, span(p)]
            for k in range(Z - 1):
                total = total + zr[g, k, :, span(p)].astype(F32)
            y16[g, :, span(p)] = total.astype(BF16)

            @pl.when(y == g % Y)
            def _():
                yown[g // Y, :, span(p)] = total

            @pl.when(y != g % Y)
            def _():
                y_copy(g, p).start()

    def over_x(c, h):
        g = 2 * c + h

        @pl.when(y == g % Y)
        def _():
            for p in range(PARTS):
                total = yown[g // Y, :, span(p)]
                for k in range(Y - 1):
                    remote(
                        y16.at[g, :, span(p)], yr.at[g // Y, k, :, span(p)],
                        y_send.at[g, p], y_recv.at[g // Y, k, p], partner,
                    ).wait_recv()
                for k in range(Y - 1):
                    total = total + yr[g // Y, k, :, span(p)].astype(F32)

                @pl.when(xh == g // Y)
                def _():
                    xown[:, span(p)] = total

                @pl.when(xh != g // Y)
                def _():
                    x16[:, span(p)] = total.astype(BF16)
                    x_copy(p).start()

    def weight_copy(f):
        part = pl.ds(pl.multiple_of(f * TILE, TILE), TILE)
        return pltpu.make_async_copy(wtile.at[lax.rem(f, W_SLOTS)], wgrad_hbm.at[part], out_sem.at[lax.rem(f, W_SLOTS)])

    def weight_tiles(first, last):
        @pl.loop(first, last)
        def _(f):
            @pl.when(f >= W_SLOTS)
            def _():
                weight_copy(f - W_SLOTS).wait()

            part = pl.ds(pl.multiple_of(f * TILE, TILE), TILE)
            product = lax.dot_general(
                srows[:, part], grad[...].reshape(2 * CHUNKS * half, width),
                (((0,), (0,)), ((), ())), preferred_element_type=F32,
            )
            wtile[lax.rem(f, W_SLOTS)] = product.astype(BF16)
            weight_copy(f).start()

    own, other = side, 1 - side

    def both(stage, c):
        stage(c, own)
        stage(c, other)

    def gap(step, place):
        if place == 0 and step + AHEAD < CHUNKS:
            logits(step + AHEAD)
        if step == 2:
            if place == 2:
                grad_copy(0, other).wait_recv()
                hidden(0, 0, 2)
            if place == 3:
                both(over_z, 0)
        if step == 3:
            if place == 0:
                both(over_y, 0)
            if place == 1:
                both(over_x, 0)
            if place == 2:
                grad_copy(1, other).wait_recv()
                hidden(1, 0, 2)
            if place == 3:
                both(over_z, 1)

    for c in range(AHEAD):
        logits(c)
    for c in range(CHUNKS):
        own_t, own_s, copies = local_stats(c)
        gap(c, 0)
        st_y[c, y] = stacked(joined(st_z, c, copies))
        copies = spread(st_y, sty_sem, c, y, [y_peer(k) for k in (1, 2, 3)])
        gap(c, 1)
        st_c[c, core] = stacked(joined(st_y, c, copies))
        copies = spread(st_c, stc_sem, c, core, [other_core])
        gap(c, 2)
        st_x[c, xh] = stacked(joined(st_c, c, copies))
        copies = spread(st_x, stx_sem, c, xh, [facing])
        gap(c, 3)
        gradient(c, own_t, own_s, joined(st_x, c, copies))

    loss_all[side] = jnp.broadcast_to(loss_row[...], (8, 128))
    loss_copy = remote(loss_all.at[side], loss_all.at[side], loss_sem.at[0], loss_sem.at[1], partner)
    loss_copy.start()
    n_f = model // TILE
    grad_copy(2, other).wait_recv()
    hidden(2, 0, 2)
    both(over_y, 1)
    hidden(3, own, 1)
    both(over_z, 2)
    both(over_x, 1)
    over_z(3, own)
    both(over_y, 2)
    grad_copy(3, other).wait_recv()
    hidden(3, other, 1)
    over_y(3, own)
    weight_tiles(0, 2)
    over_z(3, other)
    both(over_x, 2)
    over_x(3, own)
    weight_tiles(2, 6)
    over_y(3, other)
    weight_tiles(6, n_f)
    over_x(3, other)
    for p in range(PARTS):
        x_copy(p).wait_recv()
    hgrad_ref[...] = (xown[...] + xr[...].astype(F32)).astype(BF16)
    loss_copy.wait_recv()
    loss_ref[...] = jnp.sum(loss_all[0, 0:1, :] + loss_all[1, 0:1, :], axis=1, keepdims=True)

    loss_copy.wait_send()
    for copy in sent:
        copy.wait_send()
    for p in range(PARTS):
        x_copy(p).wait_send()
        for c in range(CHUNKS - SLOTS, CHUNKS):
            for h in range(2):
                core_copy(c, h, p).wait_send()
                for copy in z_copies(c, h, p):
                    copy.wait_send()

        for g in range(2 * CHUNKS):
            @pl.when(y != g % Y)
            def _():
                y_copy(g, p).wait_send()

    @pl.loop(n_f - W_SLOTS, n_f)
    def _(f):
        weight_copy(f).wait()


def shards(teacher_rows, teacher_head, student_rows, student_head, token_ids, loss_mask):
    tokens, d_t = teacher_rows.shape
    d_s, width = student_head.shape
    half = tokens // (2 * CHUNKS)
    blocks = 2 * CHUNKS
    vmem = pl.BlockSpec(memory_space=pltpu.VMEM)
    anywhere = pl.BlockSpec(memory_space=pl.ANY)
    dma = pltpu.SemaphoreType.DMA
    tiles = width // TILE
    loss, wgrad, hgrad = pl.pallas_call(
        kernel,
        out_shape=(
            jax.ShapeDtypeStruct((1, 1), F32),
            jax.ShapeDtypeStruct((d_s, width), BF16),
            jax.ShapeDtypeStruct((16, d_s), BF16),
        ),
        in_specs=[vmem, vmem, anywhere, anywhere, anywhere, anywhere],
        out_specs=(vmem, anywhere, vmem),
        scratch_shapes=[
            pltpu.VMEM((tokens, d_t), BF16),
            pltpu.VMEM((d_t, width), BF16),
            pltpu.VMEM((tokens, d_s), BF16),
            pltpu.VMEM((d_s, width), BF16),
            pltpu.VMEM((CHUNKS, 2, half, width), F32),
            pltpu.VMEM((2, half, width), F32),
            pltpu.VMEM((CHUNKS, 2, half, width), jnp.int16),
            pltpu.VMEM((CHUNKS, 2, half, width), jnp.int16),
            pltpu.VMEM((CHUNKS, 8, 128), F32),
            pltpu.VMEM((CHUNKS, 8, 128), F32),
            pltpu.VMEM((128, 128), F32),
            pltpu.VMEM((128, 128), F32),
            pltpu.VMEM((128, 128), F32),
            pltpu.VMEM((128, 128), F32),
            pltpu.VMEM((CHUNKS, Z, 8, 128), F32),
            pltpu.VMEM((CHUNKS, Y, 8, 128), F32),
            pltpu.VMEM((CHUNKS, CORES, 8, 128), F32),
            pltpu.VMEM((CHUNKS, XH, 8, 128), F32),
            pltpu.VMEM((blocks, half, width), BF16),
            pltpu.VMEM((2 * SLOTS, Z, 16, d_s), F32),
            pltpu.VMEM((2 * SLOTS, Z, 16, d_s), BF16),
            pltpu.VMEM((blocks, Z, 16, d_s), BF16),
            pltpu.VMEM((2 * SLOTS, Z, 16, d_s), BF16),
            pltpu.VMEM((blocks, Z - 1, 16, d_s), BF16),
            pltpu.VMEM((XH, 16, d_s), F32),
            pltpu.VMEM((blocks, 16, d_s), BF16),
            pltpu.VMEM((XH, Y - 1, 16, d_s), BF16),
            pltpu.VMEM((16, d_s), F32),
            pltpu.VMEM((16, d_s), BF16),
            pltpu.VMEM((16, d_s), BF16),
            pltpu.VMEM((W_SLOTS, TILE, width), BF16),
            pltpu.VMEM((1, 128), F32),
            pltpu.VMEM((2, 8, 128), F32),
            dma((2, tiles + 2)),
            dma((2, CHUNKS, 2)),
            dma((2, CHUNKS)),
            dma((2, CHUNKS, Z - 1)),
            dma((2, CHUNKS, Y - 1)),
            dma((2, CHUNKS, CORES - 1)),
            dma((2, CHUNKS, XH - 1)),
            dma((2, CHUNKS)),
            dma((2, blocks, PARTS)),
            dma((2, blocks, PARTS, Z - 1)),
            dma((blocks, PARTS)),
            dma((XH, Y - 1, PARTS)),
            dma((2, PARTS)),
            dma((2,)),
            dma((W_SLOTS,)),
        ],
        compiler_params=pltpu.CompilerParams(
            collective_id=0, has_side_effects=True, vmem_limit_bytes=60 << 20
        ),
        cost_estimate=pl.CostEstimate(flops=26_000_000_000, bytes_accessed=28_000_000, transcendentals=2_000_000),
        name="distill",
    )(
        token_ids.reshape(tokens // 128, 128),
        loss_mask.reshape(tokens // 128, 128),
        teacher_rows,
        teacher_head,
        student_rows,
        student_head,
    )
    return loss.reshape(()), wgrad, hgrad


def solution(mesh):
    placed = (P(None, "role"), P("role", "vocab"), P(None, "role"), P("role", "vocab"), P(), P())
    return jax.shard_map(
        shards,
        mesh=mesh,
        in_specs=placed,
        out_specs=(P(), P("role", "vocab"), P("vocab", "role")),
        check_vma=False,
    )
```

```python
import functools

import jax
import jax.numpy as jnp
from jax import lax
from jax.experimental import pallas as pl
from jax.experimental.pallas import tpu as pltpu
from jax.sharding import PartitionSpec as P

TAU = 2.0
BETA = 0.5
MESH = pl.DeviceIdType.MESH
F32 = jnp.float32
BF16 = jnp.bfloat16

CHUNKS = 4
AHEAD = 2
TILE = 256
LEVELS = 32767.0
XH, Y, Z, CORES = 2, 4, 4, 2
SLOTS = 3
PARTS = 2
HIDDEN_TILE = 640
W_SLOTS = 5
CARRY = 10


def as_columns(rows_ref, columns_ref):
    columns_ref[...] = rows_ref[...].T


def stacked(rows):
    place = lax.broadcasted_iota(jnp.int32, (8, 128), 0)
    tile = jnp.zeros((8, 128), F32)
    for k, row in enumerate(rows):
        tile = jnp.where(place == k, row, tile)
    return tile


def merge(tiles):
    top_t = functools.reduce(jnp.maximum, [t[0:1] for t in tiles])
    top_s = functools.reduce(jnp.maximum, [t[1:2] for t in tiles])
    teacher = cooled = student = cross = picked = 0.0
    for t in tiles:
        down_t = t[0:1] - top_t
        down_s = (t[1:2] - top_s) * 0.5
        scale_t = jnp.exp(down_t)
        scale_s = jnp.exp(down_s)
        teacher = teacher + t[2:3] * scale_t
        cooled = cooled + t[3:4] * scale_s
        student = student + t[4:5] * (scale_s * scale_s)
        cross = cross + scale_t * (t[5:6] + (down_t - down_s) * t[2:3])
        picked = picked + t[6:7]
    return top_t, top_s, teacher, cooled, student, cross, picked


def kernel(
    ids_ref, mask_ref, trows_hbm, thead_hbm, srows_hbm, shead_hbm,
    loss_ref, wgrad_hbm, hgrad_ref,
    trows, thead, srows, shead, mine, theirs, qs, qr, scale_s, scale_r, scale_columns,
    pad, columns, stat_columns, st_z, st_y, st_c, st_x, grad, h32, h16, rc, z16, zr, yown, y16, yr, xown, x16, xr,
    wtile, loss_row, loss_all,
    load_sem, q_sem, scale_sem, stz_sem, sty_sem, stc_sem, stx_sem, grad_sem, core_sem, z_sem, y_send, y_recv, x_sem,
    loss_sem, out_sem,
):
    r = lax.axis_index("role")
    v = lax.axis_index("vocab")
    core, z, y, xh = v % CORES, (v // 2) % Z, (v // 8) % Y, v // 32
    half = mine.shape[2]
    width = mine.shape[3]
    chunk = 2 * half
    model = shead.shape[0]
    tiles = width // TILE
    slab_start = v * width

    def at(role=r, x_hi=xh, yy=y, zz=z, cc=core):
        return (role, ((x_hi * Y + yy) * Z + zz) * CORES + cc)

    partner = at(role=1 - r)
    other_core = at(cc=1 - core)
    other_x = at(x_hi=1 - xh)
    side = (r + xh) % 2
    facing = at(role=1 - r, x_hi=1 - xh)

    def z_peer(k):
        return at(zz=(z + k) % Z)

    def y_peer(k):
        return at(yy=(y + k) % Y)

    def remote(src, dst, send, recv, device):
        return pltpu.make_async_remote_copy(
            src_ref=src, dst_ref=dst, send_sem=send, recv_sem=recv, device_id=device, device_id_type=MESH
        )

    sent = []

    def load_rows(m, first):
        hbm, ref = ((trows_hbm, trows), (srows_hbm, srows))[m]
        part = pl.ds(0, chunk) if first else pl.ds(chunk, ref.shape[0] - chunk)
        return pltpu.make_async_copy(hbm.at[part], ref.at[part], load_sem.at[m, tiles + (0 if first else 1)])

    def load_head(m, n):
        hbm, ref = ((thead_hbm, thead), (shead_hbm, shead))[m]
        part = pl.ds(pl.multiple_of(n * TILE, TILE), TILE)
        return pltpu.make_async_copy(hbm.at[:, part], ref.at[:, part], load_sem.at[m, n])

    load_rows(0, True).start()
    for n in range(tiles):
        load_head(0, n).start()

    barrier = pltpu.get_barrier_semaphore()
    peers = [partner, other_core, other_x, facing] + [z_peer(k) for k in (1, 2, 3)] + [y_peer(k) for k in (1, 2, 3)]
    for peer in peers:
        pl.semaphore_signal(barrier, inc=1, device_id=peer, device_id_type=MESH)

    pad[...] = jnp.zeros_like(pad)
    scale_columns[...] = jnp.zeros_like(scale_columns)
    stat_columns[...] = jnp.zeros_like(stat_columns)
    loss_row[...] = jnp.zeros_like(loss_row)

    def q_copy(c, m):
        return remote(qs.at[c, m], qr.at[c, m], q_sem.at[0, c, m], q_sem.at[1, c, m], partner)

    def scale_copy(c):
        return remote(scale_s.at[c], scale_r.at[c], scale_sem.at[0, c], scale_sem.at[1, c], partner)

    def logits(c):
        for m, (rows, head) in enumerate(((trows, thead), (srows, shead))):
            if c < 2:
                load_rows(m, c == 0).wait()

            if c == 0 and m == 0:
                load_rows(1, True).start()

            @pl.loop(0, tiles)
            def _(n):
                if c == 0:
                    load_head(m, n).wait()
                    if m == 0:
                        load_head(1, n).start()
                part = pl.ds(pl.multiple_of(n * TILE, TILE), TILE)
                product = jnp.dot(rows[pl.ds(c * chunk, chunk), :], head[:, part], preferred_element_type=F32)
                low, high = product[:half], product[half:]
                mine[c, m, :, part] = jnp.where(side == 0, low, high)
                theirs[m, :, part] = jnp.where(side == 0, high, low)

            @pl.loop(0, half // 16)
            def _(b):
                part = pl.ds(pl.multiple_of(b * 16, 16), 16)
                x = theirs[m, part, :]
                top = jnp.maximum(jnp.max(jnp.abs(x), axis=1, keepdims=True), 1e-30)
                qs[c, m, part, :] = jnp.round(x * (LEVELS / top)).astype(jnp.int32).astype(jnp.int16)
                scale_columns[part, m : m + 1] = top * (1.0 / LEVELS)

            if c == 0 and m == 0:
                for k in range(2):
                    load_rows(k, False).start()
                pl.semaphore_wait(barrier, len(peers))
            q_copy(c, m).start()
            sent.append(q_copy(c, m))
        scale_s[c] = scale_columns[...].T[0:8]
        scale_copy(c).start()
        sent.append(scale_copy(c))

    def spread(ref, sems, c, me, peer):
        copies = [
            remote(ref.at[c, me], ref.at[c, me], sems.at[0, c, k], sems.at[1, c, k], d) for k, d in enumerate(peer)
        ]
        for copy in copies:
            copy.start()
        sent.extend(copies)
        return copies

    def joined(ref, c, copies):
        for copy in copies:
            copy.wait_recv()
        return merge([ref[c, i] for i in range(ref.shape[1])])

    def local_stats(c):
        scale_copy(c).wait_recv()
        for m in range(2):
            q_copy(c, m).wait_recv()
        pad[0:8, :] = scale_r[c]
        pad[8:9, :] = ids_ref[pl.ds(2 * c + side, 1), :].astype(F32)
        as_columns(pad, columns)

        @pl.loop(0, half // 16)
        def _(b):
            part = pl.ds(pl.multiple_of(b * 16, 16), 16)
            got_t = qr[c, 0, part, :].astype(jnp.int32).astype(F32) * columns[part, 0:1]
            got_s = qr[c, 1, part, :].astype(jnp.int32).astype(F32) * columns[part, 1:2]
            t = (mine[c, 0, part, :] + got_t) * (1.0 / TAU)
            s = mine[c, 1, part, :] + got_s
            label = columns[part, 8:9].astype(jnp.int32)
            place = lax.broadcasted_iota(jnp.int32, s.shape, 1) + slab_start
            top_t = jnp.max(t, axis=1, keepdims=True)
            top_s = jnp.max(s, axis=1, keepdims=True)
            down_t = t - top_t
            down_s = (s - top_s) * (1.0 / TAU)
            exp_t = jnp.exp(down_t)
            exp_s = jnp.exp(down_s)
            mine[c, 0, part, :] = exp_t
            mine[c, 1, part, :] = exp_s
            sums = (
                top_t,
                top_s,
                jnp.sum(exp_t, axis=1, keepdims=True),
                jnp.sum(exp_s, axis=1, keepdims=True),
                jnp.sum(exp_s * exp_s, axis=1, keepdims=True),
                jnp.sum(exp_t * (down_t - down_s), axis=1, keepdims=True),
                jnp.sum(jnp.where(place == label, s, 0.0), axis=1, keepdims=True),
            )
            for k, value in enumerate(sums):
                stat_columns[part, k : k + 1] = value

        tile = stat_columns[...].T[0:8]
        st_z[c, z] = tile
        return tile[0:1], tile[1:2], spread(st_z, stz_sem, c, z, [z_peer(k) for k in (1, 2, 3)])

    def grad_copy(c, h):
        block = grad.at[2 * c + h]
        return remote(block, block, grad_sem.at[0, c], grad_sem.at[1, c], partner)

    def gradient(c, own_t, own_s, stats):
        top_t, top_s, teacher, cooled, student, cross, picked = stats
        mask = mask_ref[pl.ds(2 * c + side, 1), :].astype(F32)
        down_s = jnp.exp((own_s - top_s) * 0.5)
        pad[0:8, :] = stacked([
            TAU * mask * (down_s / cooled),
            TAU * mask * (jnp.exp(own_t - top_t) / teacher),
            BETA * mask * (down_s * down_s / student),
            BETA * mask,
        ])
        as_columns(pad, columns)
        loss_row[...] += mask * (
            TAU * TAU * (cross / teacher - jnp.log(teacher) + jnp.log(cooled))
            - BETA * (picked - top_s - jnp.log(student))
        )

        @pl.loop(0, half // 16)
        def _(b):
            part = pl.ds(pl.multiple_of(b * 16, 16), 16)
            exp_t = mine[c, 0, part, :]
            exp_s = mine[c, 1, part, :]
            label = columns[part, 8:9].astype(jnp.int32)
            place = lax.broadcasted_iota(jnp.int32, exp_s.shape, 1) + slab_start
            g = exp_s * (columns[part, 0:1] + columns[part, 2:3] * exp_s) - exp_t * columns[part, 1:2]
            g = g - jnp.where(place == label, columns[part, 3:4], 0.0)
            grad[2 * c + side, part, :] = g.astype(BF16)

        grad_copy(c, side).start()
        sent.append(grad_copy(c, side))

    def span(p):
        return pl.ds(p * (model // PARTS), model // PARTS)

    def slot_of(c, h):
        return 2 * (c % SLOTS) + h

    def core_copy(c, h, p):
        g = 2 * c + h
        return remote(
            h16.at[slot_of(c, h), :, :, span(p)], rc.at[g, :, :, span(p)],
            core_sem.at[0, g, p], core_sem.at[1, g, p], other_core,
        )

    def z_copies(c, h, p):
        g = 2 * c + h
        return [
            remote(
                z16.at[slot_of(c, h), (z + k) % Z, :, span(p)], zr.at[g, k - 1, :, span(p)],
                z_sem.at[0, g, p, k - 1], z_sem.at[1, g, p, k - 1], z_peer(k),
            )
            for k in (1, 2, 3)
        ]

    def y_copy(g, p):
        hop = (g % Y - y + Y) % Y
        return remote(
            y16.at[g, :, span(p)], yr.at[g // Y, hop - 1, :, span(p)],
            y_send.at[g, p], y_recv.at[g // Y, hop - 1, p], at(yy=g % Y),
        )

    def x_copy(p):
        return remote(x16.at[:, span(p)], xr.at[:, span(p)], x_sem.at[0, p], x_sem.at[1, p], other_x)

    def hidden(*blocks):
        count = len(blocks)
        for c, h in blocks:
            if c >= SLOTS:
                for p in range(PARTS):
                    core_copy(c - SLOTS, h, p).wait_send()
        wide = HIDDEN_TILE
        for p in range(PARTS):
            @pl.loop(0, model // PARTS // wide)
            def _(n):
                part = pl.ds(pl.multiple_of(p * (model // PARTS) + n * wide, 128), wide)
                rows = [grad[2 * c + h] for c, h in blocks]
                product = lax.dot_general(
                    rows[0] if count == 1 else jnp.concatenate(rows), shead[part, :],
                    (((1,), (1,)), ((), ())), preferred_element_type=F32,
                ).reshape(count, Z, CORES, 16, wide)
                for i, (c, h) in enumerate(blocks):
                    first, second = product[i, :, 0], product[i, :, 1]
                    h32[slot_of(c, h), :, :, part] = jnp.where(core == 0, first, second)
                    h16[slot_of(c, h), :, :, part] = jnp.where(core == 0, second, first).astype(BF16)

            for c, h in blocks:
                core_copy(c, h, p).start()

    def over_z(c, h):
        g = 2 * c + h
        slot = slot_of(c, h)
        for p in range(PARTS):
            core_copy(c, h, p).wait_recv()
            if c >= SLOTS:
                for copy in z_copies(c - SLOTS, h, p):
                    copy.wait_send()

            @pl.loop(0, Z)
            def _(i):
                total = h32[slot, i, :, span(p)] + rc[g, i, :, span(p)].astype(F32)
                h32[slot, i, :, span(p)] = total
                z16[slot, i, :, span(p)] = total.astype(BF16)

            for copy in z_copies(c, h, p):
                copy.start()

    def over_y(c, h):
        g = 2 * c + h
        for p in range(PARTS):
            for copy in z_copies(c, h, p):
                copy.wait_recv()
            total = h32[slot_of(c, h), z, :, span(p)]
            for k in range(Z - 1):
                total = total + zr[g, k, :, span(p)].astype(F32)
            y16[g, :, span(p)] = total.astype(BF16)

            @pl.when(y == g % Y)
            def _():
                yown[g // Y, :, span(p)] = total

            @pl.when(y != g % Y)
            def _():
                y_copy(g, p).start()

    def over_x(c, h):
        g = 2 * c + h

        @pl.when(y == g % Y)
        def _():
            for p in range(PARTS):
                total = yown[g // Y, :, span(p)]
                for k in range(Y - 1):
                    remote(
                        y16.at[g, :, span(p)], yr.at[g // Y, k, :, span(p)],
                        y_send.at[g, p], y_recv.at[g // Y, k, p], partner,
                    ).wait_recv()
                for k in range(Y - 1):
                    total = total + yr[g // Y, k, :, span(p)].astype(F32)

                @pl.when(xh == g // Y)
                def _():
                    xown[:, span(p)] = total

                @pl.when(xh != g // Y)
                def _():
                    x16[:, span(p)] = total.astype(BF16)
                    x_copy(p).start()

    def weight_copy(f):
        part = pl.ds(pl.multiple_of(f * TILE, TILE), TILE)
        return pltpu.make_async_copy(wtile.at[lax.rem(f, W_SLOTS)], wgrad_hbm.at[part], out_sem.at[lax.rem(f, W_SLOTS)])

    early = 2 * (CHUNKS - 1)

    def weight_sum(f, first, last):
        part = pl.ds(pl.multiple_of(f * TILE, TILE), TILE)
        return lax.dot_general(
            srows[first * half : last * half, part], grad[first:last].reshape((last - first) * half, width),
            (((0,), (0,)), ((), ())), preferred_element_type=F32,
        )

    def weight_ahead():
        @pl.loop(0, CHUNKS)
        def _(f):
            mine[f] = weight_sum(f, 0, early).reshape(2, half, width)

    def weight_tiles(first, last):
        @pl.loop(first, last)
        def _(f):
            @pl.when(f >= W_SLOTS)
            def _():
                weight_copy(f - W_SLOTS).wait()

            if first < CHUNKS:
                total = mine[f].reshape(TILE, width) + weight_sum(f, early, 2 * CHUNKS)
            else:
                total = weight_sum(f, 0, 2 * CHUNKS)
            wtile[lax.rem(f, W_SLOTS)] = total.astype(BF16)
            weight_copy(f).start()

    own, other = side, 1 - side

    def both(stage, c):
        stage(c, own)
        stage(c, other)

    def gap(step, place):
        if place == 0 and step + AHEAD < CHUNKS:
            logits(step + AHEAD)
        if (step, place) == (1, 1):
            hidden((0, own))
        if (step, place) == (1, 3):
            over_z(0, own)
        if (step, place) == (2, 0):
            hidden((1, own))
        if (step, place) == (2, 1):
            over_y(0, own)
            over_z(1, own)
        if (step, place) == (2, 3):
            grad_copy(0, other).wait_recv()
            hidden((0, other))
        if (step, place) == (2, 4):
            over_z(0, other)
            hidden((2, own))
            over_y(1, own)
            over_z(2, own)
        if (step, place) == (3, 0):
            over_y(0, other)
        if (step, place) == (3, 1):
            over_y(2, own)
        if (step, place) == (3, 3):
            grad_copy(1, other).wait_recv()
            hidden((1, other))

    for c in range(AHEAD):
        logits(c)
    for c in range(CHUNKS):
        own_t, own_s, copies = local_stats(c)
        gap(c, 0)
        st_y[c, y] = stacked(joined(st_z, c, copies))
        copies = spread(st_y, sty_sem, c, y, [y_peer(k) for k in (1, 2, 3)])
        gap(c, 1)
        st_c[c, core] = stacked(joined(st_y, c, copies))
        copies = spread(st_c, stc_sem, c, core, [other_core])
        gap(c, 2)
        st_x[c, xh] = stacked(joined(st_c, c, copies))
        copies = spread(st_x, stx_sem, c, xh, [facing])
        gap(c, 3)
        gradient(c, own_t, own_s, joined(st_x, c, copies))
        gap(c, 4)

    loss_all[side] = jnp.broadcast_to(loss_row[...], (8, 128))
    loss_copy = remote(loss_all.at[side], loss_all.at[side], loss_sem.at[0], loss_sem.at[1], partner)
    loss_copy.start()
    n_f = model // TILE
    over_z(1, other)
    hidden((3, own))
    grad_copy(2, other).wait_recv()
    hidden((2, other))
    over_z(3, own)
    over_y(1, other)
    over_z(2, other)
    weight_ahead()
    grad_copy(3, other).wait_recv()
    hidden((3, other))
    over_y(3, own)
    over_z(3, other)
    over_y(2, other)
    weight_tiles(0, CHUNKS)
    over_y(3, other)
    for c in range(CHUNKS - 1):
        both(over_x, c)
    over_x(3, own)
    weight_tiles(CHUNKS, 8)
    over_x(3, other)
    weight_tiles(8, n_f)
    for p in range(PARTS):
        x_copy(p).wait_recv()
    hgrad_ref[...] = (xown[...] + xr[...].astype(F32)).astype(BF16)
    loss_copy.wait_recv()
    loss_ref[...] = jnp.sum(loss_all[0, 0:1, :] + loss_all[1, 0:1, :], axis=1, keepdims=True)

    loss_copy.wait_send()
    for copy in sent:
        copy.wait_send()
    for p in range(PARTS):
        x_copy(p).wait_send()
        for c in range(CHUNKS - SLOTS, CHUNKS):
            for h in range(2):
                core_copy(c, h, p).wait_send()
                for copy in z_copies(c, h, p):
                    copy.wait_send()

        for g in range(2 * CHUNKS):
            @pl.when(y != g % Y)
            def _():
                y_copy(g, p).wait_send()

    @pl.loop(n_f - W_SLOTS, n_f)
    def _(f):
        weight_copy(f).wait()


def carry(src, dst, held, sems):
    rows = src.shape[0] // CARRY
    parts = [pl.ds(k * rows, rows) for k in range(CARRY)]
    into = [pltpu.make_async_copy(src.at[p], held.at[p], sems.at[0, k]) for k, p in enumerate(parts)]
    back = [pltpu.make_async_copy(held.at[p], dst.at[p], sems.at[1, k]) for k, p in enumerate(parts)]
    for copy in into:
        copy.start()
    for first, second in zip(into, back):
        first.wait()
        second.start()
    for copy in back:
        copy.wait()


def shards(teacher_rows, teacher_head, student_rows, student_head, token_ids, loss_mask):
    tokens, d_t = teacher_rows.shape
    d_s, width = student_head.shape
    half = tokens // (2 * CHUNKS)
    blocks = 2 * CHUNKS
    vmem = pl.BlockSpec(memory_space=pltpu.VMEM)
    anywhere = pl.BlockSpec(memory_space=pl.ANY)
    dma = pltpu.SemaphoreType.DMA
    tiles = width // TILE
    loss, wgrad, hgrad = pl.pallas_call(
        kernel,
        out_shape=(
            jax.ShapeDtypeStruct((1, 1), F32),
            jax.ShapeDtypeStruct((d_s, width), BF16),
            jax.ShapeDtypeStruct((16, d_s), BF16),
        ),
        in_specs=[vmem, vmem, anywhere, anywhere, anywhere, anywhere],
        out_specs=(vmem, anywhere, vmem),
        scratch_shapes=[
            pltpu.VMEM((tokens, d_t), BF16),
            pltpu.VMEM((d_t, width), BF16),
            pltpu.VMEM((tokens, d_s), BF16),
            pltpu.VMEM((d_s, width), BF16),
            pltpu.VMEM((CHUNKS, 2, half, width), F32),
            pltpu.VMEM((2, half, width), F32),
            pltpu.VMEM((CHUNKS, 2, half, width), jnp.int16),
            pltpu.VMEM((CHUNKS, 2, half, width), jnp.int16),
            pltpu.VMEM((CHUNKS, 8, 128), F32),
            pltpu.VMEM((CHUNKS, 8, 128), F32),
            pltpu.VMEM((128, 128), F32),
            pltpu.VMEM((128, 128), F32),
            pltpu.VMEM((128, 128), F32),
            pltpu.VMEM((128, 128), F32),
            pltpu.VMEM((CHUNKS, Z, 8, 128), F32),
            pltpu.VMEM((CHUNKS, Y, 8, 128), F32),
            pltpu.VMEM((CHUNKS, CORES, 8, 128), F32),
            pltpu.VMEM((CHUNKS, XH, 8, 128), F32),
            pltpu.VMEM((blocks, half, width), BF16),
            pltpu.VMEM((2 * SLOTS, Z, 16, d_s), F32),
            pltpu.VMEM((2 * SLOTS, Z, 16, d_s), BF16),
            pltpu.VMEM((blocks, Z, 16, d_s), BF16),
            pltpu.VMEM((2 * SLOTS, Z, 16, d_s), BF16),
            pltpu.VMEM((blocks, Z - 1, 16, d_s), BF16),
            pltpu.VMEM((XH, 16, d_s), F32),
            pltpu.VMEM((blocks, 16, d_s), BF16),
            pltpu.VMEM((XH, Y - 1, 16, d_s), BF16),
            pltpu.VMEM((16, d_s), F32),
            pltpu.VMEM((16, d_s), BF16),
            pltpu.VMEM((16, d_s), BF16),
            pltpu.VMEM((W_SLOTS, TILE, width), BF16),
            pltpu.VMEM((1, 128), F32),
            pltpu.VMEM((2, 8, 128), F32),
            dma((2, tiles + 2)),
            dma((2, CHUNKS, 2)),
            dma((2, CHUNKS)),
            dma((2, CHUNKS, Z - 1)),
            dma((2, CHUNKS, Y - 1)),
            dma((2, CHUNKS, CORES - 1)),
            dma((2, CHUNKS, XH - 1)),
            dma((2, CHUNKS)),
            dma((2, blocks, PARTS)),
            dma((2, blocks, PARTS, Z - 1)),
            dma((blocks, PARTS)),
            dma((XH, Y - 1, PARTS)),
            dma((2, PARTS)),
            dma((2,)),
            dma((W_SLOTS,)),
        ],
        compiler_params=pltpu.CompilerParams(
            collective_id=0, has_side_effects=True, vmem_limit_bytes=60 << 20
        ),
        cost_estimate=pl.CostEstimate(flops=26_000_000_000, bytes_accessed=28_000_000, transcendentals=2_000_000),
        name="distill",
    )(
        token_ids.reshape(tokens // 128, 128),
        loss_mask.reshape(tokens // 128, 128),
        teacher_rows,
        teacher_head,
        student_rows,
        student_head,
    )
    wgrad = pl.pallas_call(
        carry,
        out_shape=jax.ShapeDtypeStruct(wgrad.shape, wgrad.dtype),
        in_specs=[anywhere],
        out_specs=anywhere,
        scratch_shapes=[pltpu.VMEM(wgrad.shape, wgrad.dtype), dma((2, CARRY))],
        compiler_params=pltpu.CompilerParams(vmem_limit_bytes=60 << 20),
        cost_estimate=pl.CostEstimate(flops=0, bytes_accessed=2 * wgrad.size * 2, transcendentals=0),
        name="carry",
    )(wgrad)
    return loss.reshape(()), wgrad, hgrad


def solution(mesh):
    placed = (P(None, "role"), P("role", "vocab"), P(None, "role"), P("role", "vocab"), P(), P())
    return jax.shard_map(
        shards,
        mesh=mesh,
        in_specs=placed,
        out_specs=(P(), P("role", "vocab"), P("vocab", "role")),
        check_vma=False,
    )
```

```python
import functools

import jax
import jax.numpy as jnp
from jax import lax
from jax.experimental import pallas as pl
from jax.experimental.pallas import tpu as pltpu
from jax.sharding import PartitionSpec as P

TAU = 2.0
BETA = 0.5
MESH = pl.DeviceIdType.MESH
F32 = jnp.float32
BF16 = jnp.bfloat16

CHUNKS = 4
AHEAD = 2
TILE = 256
LEVELS = 32767.0
XH, Y, Z, CORES = 2, 4, 4, 2
SLOTS = 3
PARTS = 2
HIDDEN_TILE = 1280
W_TILE = 512
W_SLOTS = 3
AHEAD_TILES = 2
CARRY = 10


def as_columns(rows_ref, columns_ref):
    columns_ref[...] = rows_ref[...].T


def stacked(rows):
    place = lax.broadcasted_iota(jnp.int32, (8, 128), 0)
    tile = jnp.zeros((8, 128), F32)
    for k, row in enumerate(rows):
        tile = jnp.where(place == k, row, tile)
    return tile


def merge(tiles):
    top_t = functools.reduce(jnp.maximum, [t[0:1] for t in tiles])
    top_s = functools.reduce(jnp.maximum, [t[1:2] for t in tiles])
    teacher = cooled = student = cross = picked = 0.0
    for t in tiles:
        down_t = t[0:1] - top_t
        down_s = (t[1:2] - top_s) * 0.5
        scale_t = jnp.exp(down_t)
        scale_s = jnp.exp(down_s)
        teacher = teacher + t[2:3] * scale_t
        cooled = cooled + t[3:4] * scale_s
        student = student + t[4:5] * (scale_s * scale_s)
        cross = cross + scale_t * (t[5:6] + (down_t - down_s) * t[2:3])
        picked = picked + t[6:7]
    return top_t, top_s, teacher, cooled, student, cross, picked


def kernel(
    ids_ref, mask_ref, trows_hbm, thead_hbm, srows_hbm, shead_hbm,
    loss_ref, wgrad_hbm, hgrad_ref,
    trows, thead, srows, shead, mine, theirs, qs, qr, scale_s, scale_r, scale_columns,
    pad, columns, stat_columns, st_z, st_y, st_c, st_x, grad, h32, h16, rc, z16, zr, yown, y16, yr, xown, x16, xr,
    wtile, loss_row, loss_all,
    load_sem, q_sem, scale_sem, stz_sem, sty_sem, stc_sem, stx_sem, grad_sem, core_sem, z_sem, y_send, y_recv, x_sem,
    loss_sem, out_sem,
):
    r = lax.axis_index("role")
    v = lax.axis_index("vocab")
    core, z, y, xh = v % CORES, (v // 2) % Z, (v // 8) % Y, v // 32
    half = mine.shape[2]
    width = mine.shape[3]
    chunk = 2 * half
    model = shead.shape[0]
    tiles = width // TILE
    slab_start = v * width

    def at(role=r, x_hi=xh, yy=y, zz=z, cc=core):
        return (role, ((x_hi * Y + yy) * Z + zz) * CORES + cc)

    partner = at(role=1 - r)
    other_core = at(cc=1 - core)
    other_x = at(x_hi=1 - xh)
    side = (r + xh) % 2
    facing = at(role=1 - r, x_hi=1 - xh)

    def z_peer(k):
        return at(zz=(z + k) % Z)

    def y_peer(k):
        return at(yy=(y + k) % Y)

    def remote(src, dst, send, recv, device):
        return pltpu.make_async_remote_copy(
            src_ref=src, dst_ref=dst, send_sem=send, recv_sem=recv, device_id=device, device_id_type=MESH
        )

    sent = []

    def load_rows(m, first):
        hbm, ref = ((trows_hbm, trows), (srows_hbm, srows))[m]
        part = pl.ds(0, chunk) if first else pl.ds(chunk, ref.shape[0] - chunk)
        return pltpu.make_async_copy(hbm.at[part], ref.at[part], load_sem.at[m, tiles + (0 if first else 1)])

    def load_head(m, n):
        hbm, ref = ((thead_hbm, thead), (shead_hbm, shead))[m]
        part = pl.ds(pl.multiple_of(n * TILE, TILE), TILE)
        return pltpu.make_async_copy(hbm.at[:, part], ref.at[:, part], load_sem.at[m, n])

    load_rows(0, True).start()
    for n in range(tiles):
        load_head(0, n).start()

    barrier = pltpu.get_barrier_semaphore()
    peers = [partner, other_core, other_x, facing] + [z_peer(k) for k in (1, 2, 3)] + [y_peer(k) for k in (1, 2, 3)]
    for peer in peers:
        pl.semaphore_signal(barrier, inc=1, device_id=peer, device_id_type=MESH)

    pad[...] = jnp.zeros_like(pad)
    scale_columns[...] = jnp.zeros_like(scale_columns)
    stat_columns[...] = jnp.zeros_like(stat_columns)
    loss_row[...] = jnp.zeros_like(loss_row)

    def q_copy(c, m):
        return remote(qs.at[c, m], qr.at[c, m], q_sem.at[0, c, m], q_sem.at[1, c, m], partner)

    def scale_copy(c):
        return remote(scale_s.at[c], scale_r.at[c], scale_sem.at[0, c], scale_sem.at[1, c], partner)

    def logits(c):
        for m, (rows, head) in enumerate(((trows, thead), (srows, shead))):
            if c < 2:
                load_rows(m, c == 0).wait()

            if c == 0 and m == 0:
                load_rows(1, True).start()

            wide = TILE if c == 0 else width

            @pl.loop(0, width // wide)
            def _(n):
                if c == 0:
                    load_head(m, n).wait()
                    if m == 0:
                        load_head(1, n).start()
                part = pl.ds(pl.multiple_of(n * wide, TILE), wide)
                product = jnp.dot(rows[pl.ds(c * chunk, chunk), :], head[:, part], preferred_element_type=F32)
                low, high = product[:half], product[half:]
                mine[c, m, :, part] = jnp.where(side == 0, low, high)
                theirs[m, :, part] = jnp.where(side == 0, high, low)

            @pl.loop(0, half // 16)
            def _(b):
                part = pl.ds(pl.multiple_of(b * 16, 16), 16)
                x = theirs[m, part, :]
                top = jnp.maximum(jnp.max(jnp.abs(x), axis=1, keepdims=True), 1e-30)
                qs[c, m, part, :] = jnp.round(x * (LEVELS / top)).astype(jnp.int32).astype(jnp.int16)
                scale_columns[part, m : m + 1] = top * (1.0 / LEVELS)

            if c == 0 and m == 0:
                for k in range(2):
                    load_rows(k, False).start()
                pl.semaphore_wait(barrier, len(peers))
            q_copy(c, m).start()
            sent.append(q_copy(c, m))
        scale_s[c] = scale_columns[...].T[0:8]
        scale_copy(c).start()
        sent.append(scale_copy(c))

    def spread(ref, sems, c, me, peer):
        copies = [
            remote(ref.at[c, me], ref.at[c, me], sems.at[0, c, k], sems.at[1, c, k], d) for k, d in enumerate(peer)
        ]
        for copy in copies:
            copy.start()
        sent.extend(copies)
        return copies

    def joined(ref, c, copies):
        for copy in copies:
            copy.wait_recv()
        return merge([ref[c, i] for i in range(ref.shape[1])])

    def local_stats(c):
        scale_copy(c).wait_recv()
        for m in range(2):
            q_copy(c, m).wait_recv()
        pad[0:8, :] = scale_r[c]
        pad[8:9, :] = ids_ref[pl.ds(2 * c + side, 1), :].astype(F32)
        as_columns(pad, columns)

        @pl.loop(0, half // 16)
        def _(b):
            part = pl.ds(pl.multiple_of(b * 16, 16), 16)
            got_t = qr[c, 0, part, :].astype(jnp.int32).astype(F32) * columns[part, 0:1]
            got_s = qr[c, 1, part, :].astype(jnp.int32).astype(F32) * columns[part, 1:2]
            t = (mine[c, 0, part, :] + got_t) * (1.0 / TAU)
            s = mine[c, 1, part, :] + got_s
            label = columns[part, 8:9].astype(jnp.int32)
            place = lax.broadcasted_iota(jnp.int32, s.shape, 1) + slab_start
            top_t = jnp.max(t, axis=1, keepdims=True)
            top_s = jnp.max(s, axis=1, keepdims=True)
            down_t = t - top_t
            down_s = (s - top_s) * (1.0 / TAU)
            exp_t = jnp.exp(down_t)
            exp_s = jnp.exp(down_s)
            mine[c, 0, part, :] = exp_t
            mine[c, 1, part, :] = exp_s
            sums = (
                top_t,
                top_s,
                jnp.sum(exp_t, axis=1, keepdims=True),
                jnp.sum(exp_s, axis=1, keepdims=True),
                jnp.sum(exp_s * exp_s, axis=1, keepdims=True),
                jnp.sum(exp_t * (down_t - down_s), axis=1, keepdims=True),
                jnp.sum(jnp.where(place == label, s, 0.0), axis=1, keepdims=True),
            )
            for k, value in enumerate(sums):
                stat_columns[part, k : k + 1] = value

        tile = stat_columns[...].T[0:8]
        st_z[c, z] = tile
        return tile[0:1], tile[1:2], spread(st_z, stz_sem, c, z, [z_peer(k) for k in (1, 2, 3)])

    def grad_copy(c, h):
        block = grad.at[2 * c + h]
        return remote(block, block, grad_sem.at[0, c], grad_sem.at[1, c], partner)

    def gradient(c, own_t, own_s, stats):
        top_t, top_s, teacher, cooled, student, cross, picked = stats
        mask = mask_ref[pl.ds(2 * c + side, 1), :].astype(F32)
        down_s = jnp.exp((own_s - top_s) * 0.5)
        pad[0:8, :] = stacked([
            TAU * mask * (down_s / cooled),
            TAU * mask * (jnp.exp(own_t - top_t) / teacher),
            BETA * mask * (down_s * down_s / student),
            BETA * mask,
        ])
        as_columns(pad, columns)
        loss_row[...] += mask * (
            TAU * TAU * (cross / teacher - jnp.log(teacher) + jnp.log(cooled))
            - BETA * (picked - top_s - jnp.log(student))
        )

        @pl.loop(0, half // 16)
        def _(b):
            part = pl.ds(pl.multiple_of(b * 16, 16), 16)
            exp_t = mine[c, 0, part, :]
            exp_s = mine[c, 1, part, :]
            label = columns[part, 8:9].astype(jnp.int32)
            place = lax.broadcasted_iota(jnp.int32, exp_s.shape, 1) + slab_start
            g = exp_s * (columns[part, 0:1] + columns[part, 2:3] * exp_s) - exp_t * columns[part, 1:2]
            g = g - jnp.where(place == label, columns[part, 3:4], 0.0)
            grad[2 * c + side, part, :] = g.astype(BF16)

        grad_copy(c, side).start()
        sent.append(grad_copy(c, side))

    def span(p):
        return pl.ds(p * (model // PARTS), model // PARTS)

    def slot_of(c, h):
        return 2 * (c % SLOTS) + h

    def core_copy(c, h, p):
        g = 2 * c + h
        return remote(
            h16.at[slot_of(c, h), :, :, span(p)], rc.at[g, :, :, span(p)],
            core_sem.at[0, g, p], core_sem.at[1, g, p], other_core,
        )

    def z_copies(c, h, p):
        g = 2 * c + h
        return [
            remote(
                z16.at[slot_of(c, h), (z + k) % Z, :, span(p)], zr.at[g, k - 1, :, span(p)],
                z_sem.at[0, g, p, k - 1], z_sem.at[1, g, p, k - 1], z_peer(k),
            )
            for k in (1, 2, 3)
        ]

    def y_copy(g, p):
        hop = (g % Y - y + Y) % Y
        return remote(
            y16.at[g, :, span(p)], yr.at[g // Y, hop - 1, :, span(p)],
            y_send.at[g, p], y_recv.at[g // Y, hop - 1, p], at(yy=g % Y),
        )

    def x_copy(p):
        return remote(x16.at[:, span(p)], xr.at[:, span(p)], x_sem.at[0, p], x_sem.at[1, p], other_x)

    def hidden(*blocks):
        count = len(blocks)
        for c, h in blocks:
            if c >= SLOTS:
                for p in range(PARTS):
                    core_copy(c - SLOTS, h, p).wait_send()
        wide = HIDDEN_TILE
        for p in range(PARTS):
            @pl.loop(0, model // PARTS // wide)
            def _(n):
                part = pl.ds(pl.multiple_of(p * (model // PARTS) + n * wide, 128), wide)
                rows = [grad[2 * c + h] for c, h in blocks]
                product = lax.dot_general(
                    rows[0] if count == 1 else jnp.concatenate(rows), shead[part, :],
                    (((1,), (1,)), ((), ())), preferred_element_type=F32,
                ).reshape(count, Z, CORES, 16, wide)
                for i, (c, h) in enumerate(blocks):
                    first, second = product[i, :, 0], product[i, :, 1]
                    h32[slot_of(c, h), :, :, part] = jnp.where(core == 0, first, second)
                    h16[slot_of(c, h), :, :, part] = jnp.where(core == 0, second, first).astype(BF16)

            for c, h in blocks:
                core_copy(c, h, p).start()

    def over_z(c, h):
        g = 2 * c + h
        slot = slot_of(c, h)
        for p in range(PARTS):
            core_copy(c, h, p).wait_recv()
            if c >= SLOTS:
                for copy in z_copies(c - SLOTS, h, p):
                    copy.wait_send()

            @pl.loop(0, Z)
            def _(i):
                total = h32[slot, i, :, span(p)] + rc[g, i, :, span(p)].astype(F32)
                h32[slot, i, :, span(p)] = total
                z16[slot, i, :, span(p)] = total.astype(BF16)

            for copy in z_copies(c, h, p):
                copy.start()

    def over_y(c, h):
        g = 2 * c + h
        for p in range(PARTS):
            for copy in z_copies(c, h, p):
                copy.wait_recv()
            total = h32[slot_of(c, h), z, :, span(p)]
            for k in range(Z - 1):
                total = total + zr[g, k, :, span(p)].astype(F32)
            y16[g, :, span(p)] = total.astype(BF16)

            @pl.when(y == g % Y)
            def _():
                yown[g // Y, :, span(p)] = total

            @pl.when(y != g % Y)
            def _():
                y_copy(g, p).start()

    def over_x(c, h):
        g = 2 * c + h

        @pl.when(y == g % Y)
        def _():
            for p in range(PARTS):
                total = yown[g // Y, :, span(p)]
                for k in range(Y - 1):
                    remote(
                        y16.at[g, :, span(p)], yr.at[g // Y, k, :, span(p)],
                        y_send.at[g, p], y_recv.at[g // Y, k, p], partner,
                    ).wait_recv()
                for k in range(Y - 1):
                    total = total + yr[g // Y, k, :, span(p)].astype(F32)

                @pl.when(xh == g // Y)
                def _():
                    xown[:, span(p)] = total

                @pl.when(xh != g // Y)
                def _():
                    x16[:, span(p)] = total.astype(BF16)
                    x_copy(p).start()

    n_f = model // W_TILE
    early = 2 * (CHUNKS - 1)
    per_tile = W_TILE // (2 * half)

    def weight_copy(f):
        part = pl.ds(pl.multiple_of(f * W_TILE, W_TILE), W_TILE)
        return pltpu.make_async_copy(wtile.at[lax.rem(f, W_SLOTS)], wgrad_hbm.at[part], out_sem.at[lax.rem(f, W_SLOTS)])

    def weight_sum(f, first, last):
        part = pl.ds(pl.multiple_of(f * W_TILE, W_TILE), W_TILE)
        return lax.dot_general(
            srows[first * half : last * half, part], grad[first:last].reshape((last - first) * half, width),
            (((0,), (0,)), ((), ())), preferred_element_type=F32,
        )

    def weight_ahead():
        @pl.loop(0, AHEAD_TILES)
        def _(f):
            mine[pl.ds(f * per_tile, per_tile)] = weight_sum(f, 0, early).reshape(per_tile, 2, half, width)

    def weight_tiles(first, last):
        @pl.loop(first, last)
        def _(f):
            @pl.when(f >= W_SLOTS)
            def _():
                weight_copy(f - W_SLOTS).wait()

            if first < AHEAD_TILES:
                total = mine[pl.ds(f * per_tile, per_tile)].reshape(W_TILE, width) + weight_sum(f, early, 2 * CHUNKS)
            else:
                total = weight_sum(f, 0, 2 * CHUNKS)
            wtile[lax.rem(f, W_SLOTS)] = total.astype(BF16)
            weight_copy(f).start()

    own, other = side, 1 - side

    def both(stage, c):
        stage(c, own)
        stage(c, other)

    def gap(step, place):
        if place == 0 and step + AHEAD < CHUNKS:
            logits(step + AHEAD)
        if (step, place) == (1, 1):
            hidden((0, own))
        if (step, place) == (1, 3):
            over_z(0, own)
        if (step, place) == (2, 0):
            hidden((1, own))
        if (step, place) == (2, 1):
            over_y(0, own)
            over_z(1, own)
        if (step, place) == (2, 3):
            grad_copy(0, other).wait_recv()
            hidden((0, other))
        if (step, place) == (2, 4):
            over_z(0, other)
            hidden((2, own))
            over_y(1, own)
            over_z(2, own)
        if (step, place) == (3, 0):
            over_y(0, other)
        if (step, place) == (3, 1):
            over_y(2, own)
        if (step, place) == (3, 3):
            grad_copy(1, other).wait_recv()
            hidden((1, other))

    for c in range(AHEAD):
        logits(c)
    for c in range(CHUNKS):
        own_t, own_s, copies = local_stats(c)
        gap(c, 0)
        st_y[c, y] = stacked(joined(st_z, c, copies))
        copies = spread(st_y, sty_sem, c, y, [y_peer(k) for k in (1, 2, 3)])
        gap(c, 1)
        st_c[c, core] = stacked(joined(st_y, c, copies))
        copies = spread(st_c, stc_sem, c, core, [other_core])
        gap(c, 2)
        st_x[c, xh] = stacked(joined(st_c, c, copies))
        copies = spread(st_x, stx_sem, c, xh, [facing])
        gap(c, 3)
        gradient(c, own_t, own_s, joined(st_x, c, copies))
        gap(c, 4)

    loss_all[side] = jnp.broadcast_to(loss_row[...], (8, 128))
    loss_copy = remote(loss_all.at[side], loss_all.at[side], loss_sem.at[0], loss_sem.at[1], partner)
    loss_copy.start()
    over_z(1, other)
    grad_copy(2, other).wait_recv()
    hidden((3, own), (2, other))
    over_z(3, own)
    over_y(1, other)
    over_z(2, other)
    weight_ahead()
    grad_copy(3, other).wait_recv()
    hidden((3, other))
    over_y(3, own)
    over_z(3, other)
    over_y(2, other)
    weight_tiles(0, 2)
    over_y(3, other)
    for c in range(CHUNKS - 1):
        both(over_x, c)
    over_x(3, own)
    weight_tiles(2, 4)
    over_x(3, other)
    weight_tiles(4, n_f)
    for p in range(PARTS):
        x_copy(p).wait_recv()
    hgrad_ref[...] = (xown[...] + xr[...].astype(F32)).astype(BF16)
    loss_copy.wait_recv()
    loss_ref[...] = jnp.sum(loss_all[0, 0:1, :] + loss_all[1, 0:1, :], axis=1, keepdims=True)

    loss_copy.wait_send()
    for copy in sent:
        copy.wait_send()
    for p in range(PARTS):
        x_copy(p).wait_send()
        for c in range(CHUNKS - SLOTS, CHUNKS):
            for h in range(2):
                core_copy(c, h, p).wait_send()
                for copy in z_copies(c, h, p):
                    copy.wait_send()

        for g in range(2 * CHUNKS):
            @pl.when(y != g % Y)
            def _():
                y_copy(g, p).wait_send()

    @pl.loop(n_f - W_SLOTS, n_f)
    def _(f):
        weight_copy(f).wait()


def carry(src, dst, held, sems):
    rows = src.shape[0] // CARRY
    parts = [pl.ds(k * rows, rows) for k in range(CARRY)]
    into = [pltpu.make_async_copy(src.at[p], held.at[p], sems.at[0, k]) for k, p in enumerate(parts)]
    back = [pltpu.make_async_copy(held.at[p], dst.at[p], sems.at[1, k]) for k, p in enumerate(parts)]
    for copy in into:
        copy.start()
    for first, second in zip(into, back):
        first.wait()
        second.start()
    for copy in back:
        copy.wait()


def shards(teacher_rows, teacher_head, student_rows, student_head, token_ids, loss_mask):
    tokens, d_t = teacher_rows.shape
    d_s, width = student_head.shape
    half = tokens // (2 * CHUNKS)
    blocks = 2 * CHUNKS
    vmem = pl.BlockSpec(memory_space=pltpu.VMEM)
    anywhere = pl.BlockSpec(memory_space=pl.ANY)
    dma = pltpu.SemaphoreType.DMA
    tiles = width // TILE
    loss, wgrad, hgrad = pl.pallas_call(
        kernel,
        out_shape=(
            jax.ShapeDtypeStruct((1, 1), F32),
            jax.ShapeDtypeStruct((d_s, width), BF16),
            jax.ShapeDtypeStruct((16, d_s), BF16),
        ),
        in_specs=[vmem, vmem, anywhere, anywhere, anywhere, anywhere],
        out_specs=(vmem, anywhere, vmem),
        scratch_shapes=[
            pltpu.VMEM((tokens, d_t), BF16),
            pltpu.VMEM((d_t, width), BF16),
            pltpu.VMEM((tokens, d_s), BF16),
            pltpu.VMEM((d_s, width), BF16),
            pltpu.VMEM((CHUNKS, 2, half, width), F32),
            pltpu.VMEM((2, half, width), F32),
            pltpu.VMEM((CHUNKS, 2, half, width), jnp.int16),
            pltpu.VMEM((CHUNKS, 2, half, width), jnp.int16),
            pltpu.VMEM((CHUNKS, 8, 128), F32),
            pltpu.VMEM((CHUNKS, 8, 128), F32),
            pltpu.VMEM((128, 128), F32),
            pltpu.VMEM((128, 128), F32),
            pltpu.VMEM((128, 128), F32),
            pltpu.VMEM((128, 128), F32),
            pltpu.VMEM((CHUNKS, Z, 8, 128), F32),
            pltpu.VMEM((CHUNKS, Y, 8, 128), F32),
            pltpu.VMEM((CHUNKS, CORES, 8, 128), F32),
            pltpu.VMEM((CHUNKS, XH, 8, 128), F32),
            pltpu.VMEM((blocks, half, width), BF16),
            pltpu.VMEM((2 * SLOTS, Z, 16, d_s), F32),
            pltpu.VMEM((2 * SLOTS, Z, 16, d_s), BF16),
            pltpu.VMEM((blocks, Z, 16, d_s), BF16),
            pltpu.VMEM((2 * SLOTS, Z, 16, d_s), BF16),
            pltpu.VMEM((blocks, Z - 1, 16, d_s), BF16),
            pltpu.VMEM((XH, 16, d_s), F32),
            pltpu.VMEM((blocks, 16, d_s), BF16),
            pltpu.VMEM((XH, Y - 1, 16, d_s), BF16),
            pltpu.VMEM((16, d_s), F32),
            pltpu.VMEM((16, d_s), BF16),
            pltpu.VMEM((16, d_s), BF16),
            pltpu.VMEM((W_SLOTS, W_TILE, width), BF16),
            pltpu.VMEM((1, 128), F32),
            pltpu.VMEM((2, 8, 128), F32),
            dma((2, tiles + 2)),
            dma((2, CHUNKS, 2)),
            dma((2, CHUNKS)),
            dma((2, CHUNKS, Z - 1)),
            dma((2, CHUNKS, Y - 1)),
            dma((2, CHUNKS, CORES - 1)),
            dma((2, CHUNKS, XH - 1)),
            dma((2, CHUNKS)),
            dma((2, blocks, PARTS)),
            dma((2, blocks, PARTS, Z - 1)),
            dma((blocks, PARTS)),
            dma((XH, Y - 1, PARTS)),
            dma((2, PARTS)),
            dma((2,)),
            dma((W_SLOTS,)),
        ],
        compiler_params=pltpu.CompilerParams(
            collective_id=0, has_side_effects=True, vmem_limit_bytes=60 << 20
        ),
        cost_estimate=pl.CostEstimate(flops=26_000_000_000, bytes_accessed=28_000_000, transcendentals=2_000_000),
        name="distill",
    )(
        token_ids.reshape(tokens // 128, 128),
        loss_mask.reshape(tokens // 128, 128),
        teacher_rows,
        teacher_head,
        student_rows,
        student_head,
    )
    wgrad = pl.pallas_call(
        carry,
        out_shape=jax.ShapeDtypeStruct(wgrad.shape, wgrad.dtype),
        in_specs=[anywhere],
        out_specs=anywhere,
        scratch_shapes=[pltpu.VMEM(wgrad.shape, wgrad.dtype), dma((2, CARRY))],
        compiler_params=pltpu.CompilerParams(vmem_limit_bytes=60 << 20),
        cost_estimate=pl.CostEstimate(flops=0, bytes_accessed=2 * wgrad.size * 2, transcendentals=0),
        name="carry",
    )(wgrad)
    return loss.reshape(()), wgrad, hgrad


def solution(mesh):
    placed = (P(None, "role"), P("role", "vocab"), P(None, "role"), P("role", "vocab"), P(), P())
    return jax.shard_map(
        shards,
        mesh=mesh,
        in_specs=placed,
        out_specs=(P(), P("role", "vocab"), P("vocab", "role")),
        check_vma=False,
    )
```

```python
import functools

import jax
import jax.numpy as jnp
from jax import lax
from jax.experimental import pallas as pl
from jax.experimental.pallas import tpu as pltpu
from jax.sharding import PartitionSpec as P

TAU = 2.0
BETA = 0.5
MESH = pl.DeviceIdType.MESH
F32 = jnp.float32
BF16 = jnp.bfloat16

CHUNKS = 4
AHEAD = 2
TILE = 256
LEVELS = 32767.0
XH, Y, Z, CORES = 2, 4, 4, 2
SLOTS = 3
PARTS = 2
HIDDEN_TILE = 1280
W_TILE = 512
W_SLOTS = 3
AHEAD_TILES = 2
CARRY = 10


def as_columns(rows_ref, columns_ref):
    columns_ref[...] = rows_ref[...].T


def stacked(rows):
    place = lax.broadcasted_iota(jnp.int32, (8, 128), 0)
    tile = jnp.zeros((8, 128), F32)
    for k, row in enumerate(rows):
        tile = jnp.where(place == k, row, tile)
    return tile


def merge(tiles):
    top_t = functools.reduce(jnp.maximum, [t[0:1] for t in tiles])
    top_s = functools.reduce(jnp.maximum, [t[1:2] for t in tiles])
    teacher = cooled = student = cross = picked = 0.0
    for t in tiles:
        down_t = t[0:1] - top_t
        down_s = (t[1:2] - top_s) * 0.5
        scale_t = jnp.exp(down_t)
        scale_s = jnp.exp(down_s)
        teacher = teacher + t[2:3] * scale_t
        cooled = cooled + t[3:4] * scale_s
        student = student + t[4:5] * (scale_s * scale_s)
        cross = cross + scale_t * (t[5:6] + (down_t - down_s) * t[2:3])
        picked = picked + t[6:7]
    return top_t, top_s, teacher, cooled, student, cross, picked


def kernel(
    ids_ref, mask_ref, trows_hbm, thead_hbm, srows_hbm, shead_hbm,
    loss_ref, wgrad_hbm, hgrad_ref,
    trows, thead, srows, shead, mine, theirs, qs, qr, scale_s, scale_r, scale_columns,
    pad, columns, stat_columns, st_z, st_y, st_c, st_x, grad, h32, h16, rc, z16, zr, yown, y16, yr, xown, x16, xr,
    wtile, loss_row, loss_all,
    load_sem, q_sem, scale_sem, stz_sem, sty_sem, stc_sem, stx_sem, grad_sem, core_sem, z_sem, y_send, y_recv, x_sem,
    loss_sem, out_sem,
):
    r = lax.axis_index("role")
    v = lax.axis_index("vocab")
    core, z, y, xh = v % CORES, (v // 2) % Z, (v // 8) % Y, v // 32
    half = mine.shape[2]
    width = mine.shape[3]
    chunk = 2 * half
    model = shead.shape[0]
    tiles = width // TILE
    slab_start = v * width

    def at(role=r, x_hi=xh, yy=y, zz=z, cc=core):
        return (role, ((x_hi * Y + yy) * Z + zz) * CORES + cc)

    partner = at(role=1 - r)
    other_core = at(cc=1 - core)
    other_x = at(x_hi=1 - xh)
    side = (r + xh) % 2
    facing = at(role=1 - r, x_hi=1 - xh)

    def z_peer(k):
        return at(zz=(z + k) % Z)

    def y_peer(k):
        return at(yy=(y + k) % Y)

    def remote(src, dst, send, recv, device):
        return pltpu.make_async_remote_copy(
            src_ref=src, dst_ref=dst, send_sem=send, recv_sem=recv, device_id=device, device_id_type=MESH
        )

    sent = []

    def load_rows(m, first):
        hbm, ref = ((trows_hbm, trows), (srows_hbm, srows))[m]
        part = pl.ds(0, chunk) if first else pl.ds(chunk, ref.shape[0] - chunk)
        return pltpu.make_async_copy(hbm.at[part], ref.at[part], load_sem.at[m, tiles + (0 if first else 1)])

    def load_head(m, n):
        hbm, ref = ((thead_hbm, thead), (shead_hbm, shead))[m]
        part = pl.ds(pl.multiple_of(n * TILE, TILE), TILE)
        return pltpu.make_async_copy(hbm.at[:, part], ref.at[:, part], load_sem.at[m, n])

    load_rows(0, True).start()
    for n in range(tiles):
        load_head(0, n).start()

    barrier = pltpu.get_barrier_semaphore()
    peers = [partner, other_core, other_x, facing] + [z_peer(k) for k in (1, 2, 3)] + [y_peer(k) for k in (1, 2, 3)]
    for peer in peers:
        pl.semaphore_signal(barrier, inc=1, device_id=peer, device_id_type=MESH)

    pad[...] = jnp.zeros_like(pad)
    scale_columns[...] = jnp.zeros_like(scale_columns)
    stat_columns[...] = jnp.zeros_like(stat_columns)
    loss_row[...] = jnp.zeros_like(loss_row)

    def q_copy(c, m):
        return remote(qs.at[c, m], qr.at[c, m], q_sem.at[0, c, m], q_sem.at[1, c, m], partner)

    def scale_copy(c):
        return remote(scale_s.at[c], scale_r.at[c], scale_sem.at[0, c], scale_sem.at[1, c], partner)

    def logits(c):
        for m, (rows, head) in enumerate(((trows, thead), (srows, shead))):
            if c < 2:
                load_rows(m, c == 0).wait()

            if c == 0 and m == 0:
                load_rows(1, True).start()

            wide = TILE if c == 0 else width

            @pl.loop(0, width // wide)
            def _(n):
                if c == 0:
                    load_head(m, n).wait()
                    if m == 0:
                        load_head(1, n).start()
                part = pl.ds(pl.multiple_of(n * wide, TILE), wide)
                product = jnp.dot(rows[pl.ds(c * chunk, chunk), :], head[:, part], preferred_element_type=F32)
                low, high = product[:half], product[half:]
                mine[c, m, :, part] = jnp.where(side == 0, low, high)
                theirs[m, :, part] = jnp.where(side == 0, high, low)

            @pl.loop(0, half // 16)
            def _(b):
                part = pl.ds(pl.multiple_of(b * 16, 16), 16)
                x = theirs[m, part, :]
                top = jnp.maximum(jnp.max(jnp.abs(x), axis=1, keepdims=True), 1e-30)
                qs[c, m, part, :] = jnp.round(x * (LEVELS / top)).astype(jnp.int32).astype(jnp.int16)
                scale_columns[part, m : m + 1] = top * (1.0 / LEVELS)

            if c == 0 and m == 0:
                for k in range(2):
                    load_rows(k, False).start()
                pl.semaphore_wait(barrier, len(peers))
            q_copy(c, m).start()
            sent.append(q_copy(c, m))
        scale_s[c] = scale_columns[...].T[0:8]
        scale_copy(c).start()
        sent.append(scale_copy(c))

    def spread(ref, sems, c, me, peer):
        copies = [
            remote(ref.at[c, me], ref.at[c, me], sems.at[0, c, k], sems.at[1, c, k], d) for k, d in enumerate(peer)
        ]
        for copy in copies:
            copy.start()
        sent.extend(copies)
        return copies

    def joined(ref, c, copies):
        for copy in copies:
            copy.wait_recv()
        return merge([ref[c, i] for i in range(ref.shape[1])])

    def local_stats(c):
        scale_copy(c).wait_recv()
        for m in range(2):
            q_copy(c, m).wait_recv()
        pad[0:8, :] = scale_r[c]
        pad[8:9, :] = ids_ref[pl.ds(2 * c + side, 1), :].astype(F32)
        as_columns(pad, columns)

        @pl.loop(0, half // 16)
        def _(b):
            part = pl.ds(pl.multiple_of(b * 16, 16), 16)
            got_t = qr[c, 0, part, :].astype(jnp.int32).astype(F32) * columns[part, 0:1]
            got_s = qr[c, 1, part, :].astype(jnp.int32).astype(F32) * columns[part, 1:2]
            t = (mine[c, 0, part, :] + got_t) * (1.0 / TAU)
            s = mine[c, 1, part, :] + got_s
            label = columns[part, 8:9].astype(jnp.int32)
            place = lax.broadcasted_iota(jnp.int32, s.shape, 1) + slab_start
            top_t = jnp.max(t, axis=1, keepdims=True)
            top_s = jnp.max(s, axis=1, keepdims=True)
            down_t = t - top_t
            down_s = (s - top_s) * (1.0 / TAU)
            exp_t = jnp.exp(down_t)
            exp_s = jnp.exp(down_s)
            mine[c, 0, part, :] = exp_t
            mine[c, 1, part, :] = exp_s
            sums = (
                top_t,
                top_s,
                jnp.sum(exp_t, axis=1, keepdims=True),
                jnp.sum(exp_s, axis=1, keepdims=True),
                jnp.sum(exp_s * exp_s, axis=1, keepdims=True),
                jnp.sum(exp_t * (down_t - down_s), axis=1, keepdims=True),
                jnp.sum(jnp.where(place == label, s, 0.0), axis=1, keepdims=True),
            )
            for k, value in enumerate(sums):
                stat_columns[part, k : k + 1] = value

        tile = stat_columns[...].T[0:8]
        st_z[c, z] = tile
        return tile[0:1], tile[1:2], spread(st_z, stz_sem, c, z, [z_peer(k) for k in (1, 2, 3)])

    def grad_copy(c, h):
        block = grad.at[2 * c + h]
        return remote(block, block, grad_sem.at[0, c], grad_sem.at[1, c], partner)

    def gradient(c, own_t, own_s, stats):
        top_t, top_s, teacher, cooled, student, cross, picked = stats
        mask = mask_ref[pl.ds(2 * c + side, 1), :].astype(F32)
        down_s = jnp.exp((own_s - top_s) * 0.5)
        pad[0:8, :] = stacked([
            TAU * mask * (down_s / cooled),
            TAU * mask * (jnp.exp(own_t - top_t) / teacher),
            BETA * mask * (down_s * down_s / student),
            BETA * mask,
        ])
        as_columns(pad, columns)
        loss_row[...] += mask * (
            TAU * TAU * (cross / teacher - jnp.log(teacher) + jnp.log(cooled))
            - BETA * (picked - top_s - jnp.log(student))
        )

        @pl.loop(0, half // 16)
        def _(b):
            part = pl.ds(pl.multiple_of(b * 16, 16), 16)
            exp_t = mine[c, 0, part, :]
            exp_s = mine[c, 1, part, :]
            label = columns[part, 8:9].astype(jnp.int32)
            place = lax.broadcasted_iota(jnp.int32, exp_s.shape, 1) + slab_start
            g = exp_s * (columns[part, 0:1] + columns[part, 2:3] * exp_s) - exp_t * columns[part, 1:2]
            g = g - jnp.where(place == label, columns[part, 3:4], 0.0)
            grad[2 * c + side, part, :] = g.astype(BF16)

        grad_copy(c, side).start()
        sent.append(grad_copy(c, side))

    def span(p):
        return pl.ds(p * (model // PARTS), model // PARTS)

    def slot_of(c, h):
        return 2 * (c % SLOTS) + h

    def core_copy(c, h, p):
        g = 2 * c + h
        return remote(
            h16.at[slot_of(c, h), :, :, span(p)], rc.at[g, :, :, span(p)],
            core_sem.at[0, g, p], core_sem.at[1, g, p], other_core,
        )

    def z_copies(c, h, p):
        g = 2 * c + h
        return [
            remote(
                z16.at[slot_of(c, h), (z + k) % Z, :, span(p)], zr.at[g, k - 1, :, span(p)],
                z_sem.at[0, g, p, k - 1], z_sem.at[1, g, p, k - 1], z_peer(k),
            )
            for k in (1, 2, 3)
        ]

    def y_copy(g, p):
        hop = (g % Y - y + Y) % Y
        return remote(
            y16.at[g, :, span(p)], yr.at[g // Y, hop - 1, :, span(p)],
            y_send.at[g, p], y_recv.at[g // Y, hop - 1, p], at(yy=g % Y),
        )

    def x_copy(p):
        return remote(x16.at[:, span(p)], xr.at[:, span(p)], x_sem.at[0, p], x_sem.at[1, p], other_x)

    def hidden(*blocks):
        count = len(blocks)
        for c, h in blocks:
            if c >= SLOTS:
                for p in range(PARTS):
                    core_copy(c - SLOTS, h, p).wait_send()
        wide = HIDDEN_TILE
        for p in range(PARTS):
            @pl.loop(0, model // PARTS // wide)
            def _(n):
                part = pl.ds(pl.multiple_of(p * (model // PARTS) + n * wide, 128), wide)
                rows = [grad[2 * c + h] for c, h in blocks]
                product = lax.dot_general(
                    rows[0] if count == 1 else jnp.concatenate(rows), shead[part, :],
                    (((1,), (1,)), ((), ())), preferred_element_type=F32,
                ).reshape(count, Z, CORES, 16, wide)
                for i, (c, h) in enumerate(blocks):
                    first, second = product[i, :, 0], product[i, :, 1]
                    h32[slot_of(c, h), :, :, part] = jnp.where(core == 0, first, second)
                    h16[slot_of(c, h), :, :, part] = jnp.where(core == 0, second, first).astype(BF16)

            for c, h in blocks:
                core_copy(c, h, p).start()

    def over_z(c, h):
        g = 2 * c + h
        slot = slot_of(c, h)
        for p in range(PARTS):
            core_copy(c, h, p).wait_recv()
            if c >= SLOTS:
                for copy in z_copies(c - SLOTS, h, p):
                    copy.wait_send()

            @pl.loop(0, Z)
            def _(i):
                total = h32[slot, i, :, span(p)] + rc[g, i, :, span(p)].astype(F32)
                h32[slot, i, :, span(p)] = total
                z16[slot, i, :, span(p)] = total.astype(BF16)

            for copy in z_copies(c, h, p):
                copy.start()

    def over_y(c, h):
        g = 2 * c + h
        for p in range(PARTS):
            for copy in z_copies(c, h, p):
                copy.wait_recv()
            total = h32[slot_of(c, h), z, :, span(p)]
            for k in range(Z - 1):
                total = total + zr[g, k, :, span(p)].astype(F32)
            y16[g, :, span(p)] = total.astype(BF16)

            @pl.when(y == g % Y)
            def _():
                yown[g // Y, :, span(p)] = total

            @pl.when(y != g % Y)
            def _():
                y_copy(g, p).start()

    def over_x(c, h):
        g = 2 * c + h

        @pl.when(y == g % Y)
        def _():
            for p in range(PARTS):
                total = yown[g // Y, :, span(p)]
                for k in range(Y - 1):
                    remote(
                        y16.at[g, :, span(p)], yr.at[g // Y, k, :, span(p)],
                        y_send.at[g, p], y_recv.at[g // Y, k, p], partner,
                    ).wait_recv()
                for k in range(Y - 1):
                    total = total + yr[g // Y, k, :, span(p)].astype(F32)

                @pl.when(xh == g // Y)
                def _():
                    xown[:, span(p)] = total

                @pl.when(xh != g // Y)
                def _():
                    x16[:, span(p)] = total.astype(BF16)
                    x_copy(p).start()

    n_f = model // W_TILE
    early = 2 * (CHUNKS - 1)
    per_tile = W_TILE // (2 * half)

    def weight_copy(f):
        part = pl.ds(pl.multiple_of(f * W_TILE, W_TILE), W_TILE)
        return pltpu.make_async_copy(wtile.at[lax.rem(f, W_SLOTS)], wgrad_hbm.at[part], out_sem.at[lax.rem(f, W_SLOTS)])

    def weight_sum(f, first, last):
        part = pl.ds(pl.multiple_of(f * W_TILE, W_TILE), W_TILE)
        return lax.dot_general(
            srows[first * half : last * half, part], grad[first:last].reshape((last - first) * half, width),
            (((0,), (0,)), ((), ())), preferred_element_type=F32,
        )

    def weight_ahead():
        @pl.loop(0, AHEAD_TILES)
        def _(f):
            mine[pl.ds(f * per_tile, per_tile)] = weight_sum(f, 0, early).reshape(per_tile, 2, half, width)

    def weight_tiles(first, last):
        @pl.loop(first, last)
        def _(f):
            @pl.when(f >= W_SLOTS)
            def _():
                weight_copy(f - W_SLOTS).wait()

            if first < AHEAD_TILES:
                total = mine[pl.ds(f * per_tile, per_tile)].reshape(W_TILE, width) + weight_sum(f, early, 2 * CHUNKS)
            else:
                total = weight_sum(f, 0, 2 * CHUNKS)
            wtile[lax.rem(f, W_SLOTS)] = total.astype(BF16)
            weight_copy(f).start()

    own, other = side, 1 - side

    def both(stage, c):
        stage(c, own)
        stage(c, other)

    def gap(step, place):
        if place == 0 and step + AHEAD < CHUNKS:
            logits(step + AHEAD)
        if (step, place) == (1, 1):
            hidden((0, own))
        if (step, place) == (1, 3):
            over_z(0, own)
        if (step, place) == (2, 0):
            hidden((1, own))
        if (step, place) == (2, 1):
            over_y(0, own)
            over_z(1, own)
        if (step, place) == (2, 3):
            grad_copy(0, other).wait_recv()
            hidden((0, other))
        if (step, place) == (2, 4):
            over_z(0, other)
            hidden((2, own))
            over_y(1, own)
            over_z(2, own)
        if (step, place) == (3, 0):
            over_y(0, other)
        if (step, place) == (3, 1):
            over_y(2, own)
        if (step, place) == (3, 3):
            grad_copy(1, other).wait_recv()
            hidden((1, other))

    for c in range(AHEAD):
        logits(c)
    for c in range(CHUNKS):
        own_t, own_s, copies = local_stats(c)
        gap(c, 0)
        st_y[c, y] = stacked(joined(st_z, c, copies))
        copies = spread(st_y, sty_sem, c, y, [y_peer(k) for k in (1, 2, 3)])
        gap(c, 1)
        st_c[c, core] = stacked(joined(st_y, c, copies))
        copies = spread(st_c, stc_sem, c, core, [other_core])
        gap(c, 2)
        st_x[c, xh] = stacked(joined(st_c, c, copies))
        copies = spread(st_x, stx_sem, c, xh, [facing])
        gap(c, 3)
        gradient(c, own_t, own_s, joined(st_x, c, copies))
        gap(c, 4)

    loss_all[side] = jnp.broadcast_to(loss_row[...], (8, 128))
    loss_copy = remote(loss_all.at[side], loss_all.at[side], loss_sem.at[0], loss_sem.at[1], partner)
    loss_copy.start()
    over_z(1, other)
    grad_copy(2, other).wait_recv()
    hidden((3, own), (2, other))
    over_z(3, own)
    over_y(1, other)
    over_z(2, other)
    weight_ahead()
    grad_copy(3, other).wait_recv()
    hidden((3, other))
    over_y(3, own)
    over_z(3, other)
    over_y(2, other)
    weight_tiles(0, 2)
    over_y(3, other)
    for c in range(CHUNKS - 1):
        both(over_x, c)
    over_x(3, own)
    weight_tiles(2, 4)
    over_x(3, other)
    weight_tiles(4, n_f)
    for p in range(PARTS):
        x_copy(p).wait_recv()
    hgrad_ref[...] = (xown[...] + xr[...].astype(F32)).astype(BF16)
    loss_copy.wait_recv()
    loss_ref[...] = jnp.sum(loss_all[0, 0:1, :] + loss_all[1, 0:1, :], axis=1, keepdims=True)

    loss_copy.wait_send()
    for copy in sent:
        copy.wait_send()
    for p in range(PARTS):
        x_copy(p).wait_send()
        for c in range(CHUNKS - SLOTS, CHUNKS):
            for h in range(2):
                core_copy(c, h, p).wait_send()
                for copy in z_copies(c, h, p):
                    copy.wait_send()

        for g in range(2 * CHUNKS):
            @pl.when(y != g % Y)
            def _():
                y_copy(g, p).wait_send()

    @pl.loop(n_f - W_SLOTS, n_f)
    def _(f):
        weight_copy(f).wait()


def carry(src, small_src, dst, small_dst, held, small_held, sems, small_sems):
    small_into = pltpu.make_async_copy(small_src, small_held, small_sems.at[0])
    small_back = pltpu.make_async_copy(small_held, small_dst, small_sems.at[1])
    small_into.start()
    rows = src.shape[0] // CARRY
    parts = [pl.ds(k * rows, rows) for k in range(CARRY)]
    into = [pltpu.make_async_copy(src.at[p], held.at[p], sems.at[0, k]) for k, p in enumerate(parts)]
    back = [pltpu.make_async_copy(held.at[p], dst.at[p], sems.at[1, k]) for k, p in enumerate(parts)]
    for copy in into:
        copy.start()
    for first, second in zip(into, back):
        first.wait()
        second.start()
    small_into.wait()
    small_back.start()
    for copy in back:
        copy.wait()
    small_back.wait()


def shards(teacher_rows, teacher_head, student_rows, student_head, token_ids, loss_mask):
    tokens, d_t = teacher_rows.shape
    d_s, width = student_head.shape
    half = tokens // (2 * CHUNKS)
    blocks = 2 * CHUNKS
    vmem = pl.BlockSpec(memory_space=pltpu.VMEM)
    anywhere = pl.BlockSpec(memory_space=pl.ANY)
    dma = pltpu.SemaphoreType.DMA
    tiles = width // TILE
    loss, wgrad, hgrad = pl.pallas_call(
        kernel,
        out_shape=(
            jax.ShapeDtypeStruct((1, 1), F32),
            jax.ShapeDtypeStruct((d_s, width), BF16),
            jax.ShapeDtypeStruct((16, d_s), BF16),
        ),
        in_specs=[vmem, vmem, anywhere, anywhere, anywhere, anywhere],
        out_specs=(vmem, anywhere, vmem),
        scratch_shapes=[
            pltpu.VMEM((tokens, d_t), BF16),
            pltpu.VMEM((d_t, width), BF16),
            pltpu.VMEM((tokens, d_s), BF16),
            pltpu.VMEM((d_s, width), BF16),
            pltpu.VMEM((CHUNKS, 2, half, width), F32),
            pltpu.VMEM((2, half, width), F32),
            pltpu.VMEM((CHUNKS, 2, half, width), jnp.int16),
            pltpu.VMEM((CHUNKS, 2, half, width), jnp.int16),
            pltpu.VMEM((CHUNKS, 8, 128), F32),
            pltpu.VMEM((CHUNKS, 8, 128), F32),
            pltpu.VMEM((128, 128), F32),
            pltpu.VMEM((128, 128), F32),
            pltpu.VMEM((128, 128), F32),
            pltpu.VMEM((128, 128), F32),
            pltpu.VMEM((CHUNKS, Z, 8, 128), F32),
            pltpu.VMEM((CHUNKS, Y, 8, 128), F32),
            pltpu.VMEM((CHUNKS, CORES, 8, 128), F32),
            pltpu.VMEM((CHUNKS, XH, 8, 128), F32),
            pltpu.VMEM((blocks, half, width), BF16),
            pltpu.VMEM((2 * SLOTS, Z, 16, d_s), F32),
            pltpu.VMEM((2 * SLOTS, Z, 16, d_s), BF16),
            pltpu.VMEM((blocks, Z, 16, d_s), BF16),
            pltpu.VMEM((2 * SLOTS, Z, 16, d_s), BF16),
            pltpu.VMEM((blocks, Z - 1, 16, d_s), BF16),
            pltpu.VMEM((XH, 16, d_s), F32),
            pltpu.VMEM((blocks, 16, d_s), BF16),
            pltpu.VMEM((XH, Y - 1, 16, d_s), BF16),
            pltpu.VMEM((16, d_s), F32),
            pltpu.VMEM((16, d_s), BF16),
            pltpu.VMEM((16, d_s), BF16),
            pltpu.VMEM((W_SLOTS, W_TILE, width), BF16),
            pltpu.VMEM((1, 128), F32),
            pltpu.VMEM((2, 8, 128), F32),
            dma((2, tiles + 2)),
            dma((2, CHUNKS, 2)),
            dma((2, CHUNKS)),
            dma((2, CHUNKS, Z - 1)),
            dma((2, CHUNKS, Y - 1)),
            dma((2, CHUNKS, CORES - 1)),
            dma((2, CHUNKS, XH - 1)),
            dma((2, CHUNKS)),
            dma((2, blocks, PARTS)),
            dma((2, blocks, PARTS, Z - 1)),
            dma((blocks, PARTS)),
            dma((XH, Y - 1, PARTS)),
            dma((2, PARTS)),
            dma((2,)),
            dma((W_SLOTS,)),
        ],
        compiler_params=pltpu.CompilerParams(
            collective_id=0, has_side_effects=True, vmem_limit_bytes=60 << 20
        ),
        cost_estimate=pl.CostEstimate(flops=26_000_000_000, bytes_accessed=28_000_000, transcendentals=2_000_000),
        name="distill",
    )(
        token_ids.reshape(tokens // 128, 128),
        loss_mask.reshape(tokens // 128, 128),
        teacher_rows,
        teacher_head,
        student_rows,
        student_head,
    )
    wgrad, hgrad = pl.pallas_call(
        carry,
        out_shape=tuple(jax.ShapeDtypeStruct(a.shape, a.dtype) for a in (wgrad, hgrad)),
        in_specs=[anywhere, anywhere],
        out_specs=(anywhere, anywhere),
        scratch_shapes=[
            pltpu.VMEM(wgrad.shape, wgrad.dtype), pltpu.VMEM(hgrad.shape, hgrad.dtype), dma((2, CARRY)), dma((2,)),
        ],
        compiler_params=pltpu.CompilerParams(vmem_limit_bytes=60 << 20),
        cost_estimate=pl.CostEstimate(flops=0, bytes_accessed=2 * wgrad.size * 2, transcendentals=0),
        name="carry",
    )(wgrad, hgrad)
    return loss.reshape(()), wgrad, hgrad


def solution(mesh):
    placed = (P(None, "role"), P("role", "vocab"), P(None, "role"), P("role", "vocab"), P(), P())
    return jax.shard_map(
        shards,
        mesh=mesh,
        in_specs=placed,
        out_specs=(P(), P("role", "vocab"), P("vocab", "role")),
        check_vma=False,
    )
```
